512 devices in a mesh: seq: 16 (over y, core), label: 32 (over x, z).
Axes of the slice: x: 4, y: 8, z: 8, core: 2. Of those that a mesh axis runs over, the one named last changes fastest.
Arguments:
- hidden_states: bfloat16 [4096, 4096], P('seq', 'label'), may hold values from -6 to 6
- key_weight: bfloat16 [4096, 512], P('label'), may hold values from -0.09375 to 0.09375
- queries: bfloat16 [512, 32768], P('seq', 'label'), may hold values from -18 to 18
- output_weight: bfloat16 [512, 32768], P('seq', 'label'), may hold values from -0.59765625 to 0.59765625
- code_bias: float32 [32768], P('label'), may hold values from -6 to 6
- record_ids: int32 [4096], P('seq'), may hold values from 0 to 3, never falling along the last dimension, each value on 1 to 2048 neighbouring positions
- code_labels: int32 [4, 32768], P(None, 'label'), may hold values 0 or 1
Outputs:
- code_loss: float32 [4, 32768], P(None, 'label')
- grad_queries: float32 [512, 32768], P('seq', 'label')
- grad_output: float32 [512, 32768], P('seq', 'label')
- grad_bias: float32 [32768], P('label')
- grad_key_weight: float32 [4096, 512], P('label')
The draws below stay inside these ranges and needn't reach their ends.
Inputs may be any that keep to these rules, and one draw needn't show every extreme that they name: `record_ids`: record ids never fall; every record has 1 to 2048 tokens, one exactly 2048.
All inputs are finite; a program needn't handle non-finite values. No bound on the sum of `code_labels` on one device may be relied on, other than what follows from the above.
Results may differ from the reference program's by a relative error of at most 0.015.
The reference program's roundings to bfloat16 on the way (of `keys`) count: a program that leaves them out, or rounds other values in their place, can miss the bound.
Values may be sent and summed in bfloat16 or wider, within the bound.
No kernel may reach another device: no remote copies, remote signals or barrier semaphores. Data moves between devices by JAX's collectives and lax.ppermute only.
A program may use at most 64 MiB of HBM per device.

```python
import math
import jax
import jax.numpy as jnp
import numpy as np
from jax import lax

D = 4096
Q = 512
RECORDS = 4
SEQ = 4096
CODES = 32768


def draw_queries(key, part):
    key = jax.random.fold_in(key, 11)
    entry_key, scale_key = jax.random.split(key)
    low, high = (jnp.log(0.03), jnp.log(0.3))
    scales = jnp.exp(jax.random.uniform(scale_key, (1, CODES), jnp.float32, low, high))
    entries = jnp.clip(jax.random.normal(entry_key, (Q, CODES), jnp.float32), -3.0, 3.0)
    return (entries * scales).astype(jnp.bfloat16)


def plant(values, rng, smallest, high):
    dims = values.shape
    index_at = [jax.random.randint(jax.random.fold_in(rng, axis), (), 0, dims[axis]) for axis in range(len(dims))]
    values = values.at[tuple(index_at)].set(smallest)
    longest = dims.index(max(dims))
    index_at[longest] = (index_at[longest] + 1) % dims[longest]
    return values.at[tuple(index_at)].set(high)


def level_of(key, dims, shards, least, top_value):
    loudness, own = 1.0, jax.random.fold_in(key, 6)
    for position, shards_of in shards:
        steps = jnp.exp(jax.random.uniform(jax.random.fold_in(own, position), (shards_of,), jnp.float32, least / len(shards), top_value / len(shards)))
        loudness = loudness * jnp.repeat(steps, dims[position] // shards_of).reshape([-1 if axis == position else 1 for axis in range(len(dims))])
    return loudness


def length_profile(number_of, total, most, slope):
    loads = [(1 << 20) // math.isqrt(standing ** slope) + 1 for standing in range(2, number_of + 1)]
    surplus, given = total - most - (number_of - 1), [1] * (number_of - 1)
    while surplus > 0:
        free = [i for i in range(number_of - 1) if given[i] < most]
        mass, budget = sum([loads[i] for i in free]), surplus
        for i in free:
            addition = min(most - given[i], max(1, budget * loads[i] // mass), surplus)
            given[i] = given[i] + addition
            surplus = surplus - addition
    return np.array([most] + given)


def uneven_parts(own_key, count, total, most, slope):
    if count == 2:
        one = jax.random.randint(own_key, (), max(1, total - most), min(most, total - 1) + 1)
        return jnp.stack([one, total - one])
    tallies = jnp.asarray(length_profile(count, total, most, slope), jnp.int32)
    pairs = (count - 1) // 2
    donor, taker = tallies[1:1 + 2 * pairs:2], tallies[2:2 + 2 * pairs:2]
    room = jnp.minimum(donor - 1, most - taker)
    passed = jax.random.randint(jax.random.fold_in(own_key, 1), (pairs,), 0, 1 << 20) % (room + 1)
    tallies = tallies.at[1:1 + 2 * pairs:2].set(donor - passed).at[2:2 + 2 * pairs:2].set(taker + passed)
    return tallies[jax.random.permutation(jax.random.fold_in(own_key, 2), count)]


def bell_draw(key, dims, scale, most, shards=(), kind=jnp.bfloat16):
    values = scale * jax.random.normal(key, dims, jnp.float32)
    if shards:
        values = values * level_of(key, dims, shards, -0.22, 0.18)
    return jnp.clip(values, -most, most).astype(kind)


def setup_inputs(seed: int = 0) -> dict:
    splits = jax.random.split(jax.random.key(seed), 8)
    return {
        "hidden_states": bell_draw(splits[0], (SEQ, D), 1.0, 6.0, ((0, 16), (1, 32))),
        "key_weight": bell_draw(splits[1], (D, Q), D ** -0.5, 0.09375, ((0, 32),)),
        "queries": draw_queries(jax.random.fold_in(splits[7], 71), 0),
        "output_weight": bell_draw(splits[3], (Q, CODES), 0.1, 0.59765625, ((0, 16), (1, 32))),
        "code_bias": bell_draw(splits[4], (CODES,), 1.0, 6.0, ((0, 32),), jnp.float32),
        "record_ids": jnp.searchsorted(jnp.cumsum(uneven_parts(splits[5], RECORDS, SEQ, SEQ // 2, 2)), jnp.arange(SEQ), side="right").astype(jnp.int32),
        "code_labels": plant((jax.random.randint(splits[6], (RECORDS, CODES), 0, 8) < 1).astype(jnp.int32), jax.random.fold_in(splits[6], 1), 0, 1),
    }


def reference(hidden_states, key_weight, queries, output_weight, code_bias, record_ids, code_labels):
    keys = jnp.tanh(jnp.dot(hidden_states, key_weight, preferred_element_type=jnp.float32)).astype(jnp.bfloat16)
    member = record_ids[:, None] == jnp.arange(RECORDS, dtype=jnp.int32)[None, :]
    onehot = member.astype(jnp.float32)
    span_codes = min(1024, CODES)
    block_count = CODES // span_codes
    query_blocks = queries.reshape(Q, block_count, span_codes).transpose(1, 0, 2)
    output_blocks = output_weight.reshape(Q, block_count, span_codes).transpose(1, 0, 2)
    bias_blocks = code_bias.reshape(block_count, span_codes)
    label_blocks = code_labels.reshape(RECORDS, block_count, span_codes).transpose(1, 0, 2)
    highest = lax.Precision.HIGHEST

    def scan_step(key_grad, items):
        query_blk, output_blk, bias_blk, label_blk = items
        score_vals = jnp.dot(keys, query_blk, preferred_element_type=jnp.float32)
        value_vals = jnp.dot(keys, output_blk, preferred_element_type=jnp.float32)
        record_top = jnp.stack([jnp.max(jnp.where(member[:, rec:rec + 1], score_vals, -1e30), axis=0) for rec in range(RECORDS)])
        expo = jnp.exp(score_vals - jnp.dot(onehot, record_top, precision=highest))
        denoms = jnp.dot(onehot.T, expo, precision=highest)
        numers = jnp.dot(onehot.T, expo * value_vals, precision=highest)
        pooled = numers / denoms
        logits = pooled + bias_blk[None, :]
        labels_f = label_blk.astype(jnp.float32)
        loss_blk = jax.nn.softplus(logits) - labels_f * logits
        delta = jax.nn.sigmoid(logits) - labels_f
        attend = expo / jnp.dot(onehot, denoms, precision=highest)
        pool_weight = jnp.dot(onehot, delta, precision=highest) * attend
        pool_grad = pool_weight.astype(jnp.bfloat16)
        score_grad = (pool_weight * (value_vals - jnp.dot(onehot, pooled, precision=highest))).astype(jnp.bfloat16)
        contract_rows = (((0,), (0,)), ((), ()))
        contract_cols = (((1,), (1,)), ((), ()))
        grad_out_blk = lax.dot_general(keys, pool_grad, contract_rows, preferred_element_type=jnp.float32)
        grad_query_blk = lax.dot_general(keys, score_grad, contract_rows, preferred_element_type=jnp.float32)
        key_grad = key_grad + lax.dot_general(score_grad, query_blk, contract_cols, preferred_element_type=jnp.float32)
        key_grad = key_grad + lax.dot_general(pool_grad, output_blk, contract_cols, preferred_element_type=jnp.float32)
        return key_grad, (loss_blk, grad_query_blk, grad_out_blk, jnp.sum(delta, axis=0))

    key_grad, results = lax.scan(scan_step, jnp.zeros((SEQ, Q), jnp.float32), (query_blocks, output_blocks, bias_blocks, label_blocks))
    loss_all, grad_q, grad_o, grad_b = results
    code_loss = loss_all.transpose(1, 0, 2).reshape(RECORDS, CODES)
    grad_queries = grad_q.transpose(1, 0, 2).reshape(Q, CODES)
    grad_output = grad_o.transpose(1, 0, 2).reshape(Q, CODES)
    grad_bias = grad_b.reshape(CODES)
    keys_f = keys.astype(jnp.float32)
    pre_grad = (key_grad * (1.0 - keys_f * keys_f)).astype(jnp.bfloat16)
    grad_key_weight = lax.dot_general(hidden_states, pre_grad, (((0,), (0,)), ((), ())), preferred_element_type=jnp.float32)
    return (code_loss, grad_queries, grad_output, grad_bias, grad_key_weight)
```

```python
import jax
import jax.numpy as jnp
from jax import lax
from jax.experimental import pallas as pl
from jax.experimental.pallas import tpu as pltpu
from jax.sharding import PartitionSpec as P

FAR = -1e30
ROWS = (((0,), (0,)), ((), ()))
COLS = (((1,), (1,)), ((), ()))
SPAN = 256


def keys_kernel(parts_ref, out_ref):
    own = jnp.tanh(jnp.sum(parts_ref[...], axis=0)).astype(out_ref.dtype)
    out_ref[...] = jnp.broadcast_to(own[None], out_ref.shape)


def products(keys, query_ref, output_ref):
    query_blk = query_ref[...].reshape(-1, query_ref.shape[-1])
    output_blk = output_ref[...].reshape(-1, output_ref.shape[-1])
    score_vals = jnp.dot(keys, query_blk, preferred_element_type=jnp.float32)
    value_vals = jnp.dot(keys, output_blk, preferred_element_type=jnp.float32)
    return score_vals, value_vals, query_blk, output_blk


def spread(masks, rows):
    spread_vals = rows[-1]
    for mask, row in zip(masks[:-1], rows[:-1]):
        spread_vals = jnp.where(mask, row, spread_vals)
    return spread_vals


def totals_kernel(records, keys_ref, query_ref, output_ref, ids_ref, out_ref):
    score_vals, value_vals, _, _ = products(keys_ref[...], query_ref, output_ref)
    ids = ids_ref[...]
    masks = [ids == rec for rec in range(records)]
    tops = [
        jnp.max(jnp.where(mask, score_vals, FAR), axis=0, keepdims=True) for mask in masks
    ]
    expo = jnp.exp(score_vals - spread(masks, tops))
    weighted = expo * value_vals
    logs, means = [], []
    for mask, top in zip(masks, tops):
        denom = jnp.sum(jnp.where(mask, expo, 0.0), axis=0, keepdims=True)
        numer = jnp.sum(jnp.where(mask, weighted, 0.0), axis=0, keepdims=True)
        some = denom > 0.0
        safe = jnp.where(some, denom, 1.0)
        logs.append(jnp.where(some, top + jnp.log(safe), FAR))
        means.append(jnp.where(some, numer / safe, 0.0))
    table = jnp.concatenate(logs + means, axis=0)
    out_ref[...] = jnp.broadcast_to(table[None], out_ref.shape)


def grads_kernel(
    records,
    keys_ref,
    query_ref,
    output_ref,
    ids_ref,
    totals_ref,
    bias_ref,
    labels_ref,
    loss_ref,
    bias_grad_ref,
    grads_ref,
    key_grad_ref,
    sum_ref,
):
    step = pl.program_id(0)
    keys = keys_ref[...]
    score_vals, value_vals, query_blk, output_blk = products(keys, query_ref, output_ref)
    logs, pools = [], []
    for rec in range(records):
        log_parts = totals_ref[:, rec, :]
        mean_parts = totals_ref[:, records + rec, :]
        top = jnp.max(log_parts, axis=0, keepdims=True)
        weights = jnp.exp(log_parts - top)
        denom = jnp.sum(weights, axis=0, keepdims=True)
        logs.append(top + jnp.log(denom))
        pools.append(jnp.sum(weights * mean_parts, axis=0, keepdims=True) / denom)
    logits = jnp.concatenate(pools, axis=0) + bias_ref[...]
    labels_f = labels_ref[...].astype(jnp.float32)
    small = jnp.exp(-jnp.abs(logits))
    loss_ref[...] = jnp.maximum(logits, 0.0) + jnp.log1p(small) - labels_f * logits
    delta = jnp.where(logits >= 0.0, 1.0, small) / (1.0 + small) - labels_f
    bias_grad_ref[...] = jnp.sum(delta, axis=0, keepdims=True)
    ids = ids_ref[...]
    masks = [ids == rec for rec in range(records)]
    deltas = [delta[rec : rec + 1] for rec in range(records)]
    pool_weight = spread(masks, deltas) * jnp.exp(score_vals - spread(masks, logs))
    pool_grad = pool_weight.astype(jnp.bfloat16)
    score_grad = (pool_weight * (value_vals - spread(masks, pools))).astype(jnp.bfloat16)
    shape = (grads_ref.shape[0], grads_ref.shape[2], grads_ref.shape[3])
    grads_ref[:, 0] = lax.dot_general(
        keys, score_grad, ROWS, preferred_element_type=jnp.float32
    ).reshape(shape)
    grads_ref[:, 1] = lax.dot_general(
        keys, pool_grad, ROWS, preferred_element_type=jnp.float32
    ).reshape(shape)
    part = lax.dot_general(score_grad, query_blk, COLS, preferred_element_type=jnp.float32)
    part += lax.dot_general(pool_grad, output_blk, COLS, preferred_element_type=jnp.float32)

    @pl.when(step == 0)
    def _():
        sum_ref[...] = part

    @pl.when(step > 0)
    def _():
        sum_ref[...] += part

    @pl.when(step == pl.num_programs(0) - 1)
    def _():
        key_grad_ref[...] = sum_ref[...].astype(key_grad_ref.dtype)


def pre_grad_kernel(parts_ref, keys_ref, out_ref):
    keys_f = keys_ref[...].astype(jnp.float32)
    total = jnp.sum(parts_ref[...].astype(jnp.float32), axis=0)
    own = (total * (1.0 - keys_f * keys_f)).astype(out_ref.dtype)
    out_ref[...] = jnp.broadcast_to(own[None], out_ref.shape)


def sum_kernel(parts_ref, out_ref):
    own = jnp.sum(parts_ref[...].astype(jnp.float32), axis=0).astype(out_ref.dtype)
    out_ref[...] = jnp.broadcast_to(own[None], out_ref.shape)


def swap(parts, axis):
    return lax.all_to_all(parts, axis, 0, 0, tiled=True)


def struct(shape, dtype):
    return jax.ShapeDtypeStruct(shape, dtype)


def on_device(
    hidden_states, key_weight, queries, output_weight, code_bias, record_ids, code_labels
):
    f32, bf16 = jnp.float32, jnp.bfloat16
    records, width = code_labels.shape
    seq, label = lax.axis_size("seq"), lax.axis_size("label")
    tokens, feats = hidden_states.shape
    dims = key_weight.shape[1]
    rows = queries.shape[0]
    own_toks, own_feats = tokens // label, feats // seq

    vectors = lax.all_gather(jnp.stack([queries, output_weight]), "seq", axis=0)
    partial_pre = jnp.dot(hidden_states, key_weight, preferred_element_type=f32)
    pre_parts = swap(partial_pre.reshape(label, own_toks, dims), "label")
    keys_copies = pl.pallas_call(
        keys_kernel, out_shape=struct((label, own_toks, dims), bf16)
    )(pre_parts)
    keys_own = keys_copies[0]
    keys_all = swap(keys_copies, "label").reshape(tokens, dims)

    ids = record_ids[:, None]
    span = min(SPAN, width)
    grid = (width // span,)
    whole = lambda *shape: pl.BlockSpec(shape, lambda i: (0,) * len(shape))
    codes = lambda lead: pl.BlockSpec((lead, span), lambda i: (0, i))
    vector_specs = [
        pl.BlockSpec((seq, None, rows, span), lambda i: (0, 0, 0, i)),
        pl.BlockSpec((seq, None, rows, span), lambda i: (0, 1, 0, i)),
    ]
    totals_spec = pl.BlockSpec((seq, 2 * records, span), lambda i: (0, 0, i))
    params = pltpu.CompilerParams(vmem_limit_bytes=48 * 1024 * 1024)
    totals = pl.pallas_call(
        lambda *refs: totals_kernel(records, *refs),
        grid=grid,
        in_specs=[whole(tokens, dims), *vector_specs, whole(tokens, 1)],
        out_specs=totals_spec,
        out_shape=struct((seq, 2 * records, width), f32),
        compiler_params=params,
    )(keys_all, vectors, vectors, ids)
    totals = swap(totals, "seq")

    code_loss, grad_bias, grads, key_grad = pl.pallas_call(
        lambda *refs: grads_kernel(records, *refs),
        grid=grid,
        in_specs=[
            whole(tokens, dims),
            *vector_specs,
            whole(tokens, 1),
            totals_spec,
            codes(1),
            codes(records),
        ],
        out_specs=[
            codes(records),
            codes(1),
            pl.BlockSpec((seq, 2, rows, span), lambda i: (0, 0, 0, i)),
            whole(tokens, dims),
        ],
        out_shape=[
            struct((records, width), f32),
            struct((1, width), f32),
            struct((seq, 2, rows, width), f32),
            struct((tokens, dims), bf16),
        ],
        scratch_shapes=[pltpu.VMEM((tokens, dims), f32)],
        compiler_params=params,
    )(keys_all, vectors, vectors, ids, totals, code_bias[None], code_labels)

    grads = lax.psum_scatter(grads, "seq", scatter_dimension=0)
    grad_queries, grad_output = grads[0], grads[1]

    key_parts = swap(key_grad.reshape(label, own_toks, dims), "label")
    pre_copies = pl.pallas_call(
        pre_grad_kernel, out_shape=struct((label, own_toks, dims), bf16)
    )(key_parts, keys_own)
    pre_grad = swap(pre_copies, "label").reshape(tokens, dims)
    weight_part = lax.dot_general(
        hidden_states, pre_grad, ROWS, preferred_element_type=f32
    ).astype(bf16)
    weight_parts = swap(weight_part.reshape(seq, own_feats, dims), "seq")
    weight_copies = pl.pallas_call(
        sum_kernel, out_shape=struct((seq, own_feats, dims), bf16)
    )(weight_parts)
    grad_key_weight = swap(weight_copies, "seq").reshape(feats, dims).astype(f32)
    return (code_loss, grad_queries, grad_output, grad_bias[0], grad_key_weight)


def solution(mesh):
    return jax.shard_map(
        on_device,
        mesh=mesh,
        in_specs=(
            P("seq", "label"),
            P("label", None),
            P("seq", "label"),
            P("seq", "label"),
            P("label"),
            P("seq"),
            P(None, "label"),
        ),
        out_specs=(
            P(None, "label"),
            P("seq", "label"),
            P("seq", "label"),
            P("label"),
            P("label", None),
        ),
        check_vma=False,
    )
```

```python
import jax
import jax.numpy as jnp
from jax import lax
from jax.experimental import pallas as pl
from jax.experimental.pallas import tpu as pltpu
from jax.sharding import PartitionSpec as P

FAR = -1e30
ROWS = (((0,), (0,)), ((), ()))
COLS = (((1,), (1,)), ((), ()))
SPAN = 512
LANES = 128
TAIL = 8


def fetch(vectors_ref, held_ref, sems):
    blocks = []
    for low in range(0, held_ref.shape[-1], SPAN):
        codes = slice(low, low + SPAN)
        copy = pltpu.make_async_copy(
            vectors_ref.at[:, :, :, codes], held_ref.at[:, :, :, codes], sems.at[low // SPAN]
        )
        copy.start()
        blocks.append((codes, copy))
    return blocks


def products(keys, held_ref, codes):
    query_blk = held_ref[:, 0, :, codes].reshape(-1, SPAN)
    output_blk = held_ref[:, 1, :, codes].reshape(-1, SPAN)
    score_vals = jnp.dot(keys, query_blk, preferred_element_type=jnp.float32)
    value_vals = jnp.dot(keys, output_blk, preferred_element_type=jnp.float32)
    return score_vals, value_vals, query_blk, output_blk


def spread(masks, rows):
    spread_vals = rows[-1]
    for mask, row in zip(masks[:-1], rows[:-1]):
        spread_vals = jnp.where(mask, row, spread_vals)
    return spread_vals


def pick(wanted, rows):
    return spread([wanted == rec for rec in range(len(rows))], rows)


def totals_kernel(
    records,
    keys_ref,
    vectors_ref,
    ids_ref,
    own_ref,
    out_ref,
    held_ref,
    sems,
):
    blocks = fetch(vectors_ref, held_ref, sems)
    keys = keys_ref[...]
    ids = ids_ref[...]
    masks = [ids == rec for rec in range(records)]
    first, last = ids[:1], ids[-1:]
    single = first == last
    width = own_ref.shape[1]
    for codes, copy in blocks:
        copy.wait()
        score_vals, value_vals, _, _ = products(keys, held_ref, codes)
        tops = [
            jnp.max(jnp.where(mask, score_vals, FAR), axis=0, keepdims=True) for mask in masks
        ]
        expo = jnp.exp(score_vals - spread(masks, tops))
        weighted = expo * value_vals
        logs, means = [], []
        for mask, top in zip(masks, tops):
            denom = jnp.sum(jnp.where(mask, expo, 0.0), axis=0, keepdims=True)
            numer = jnp.sum(jnp.where(mask, weighted, 0.0), axis=0, keepdims=True)
            some = denom > 0.0
            safe = jnp.where(some, denom, 1.0)
            logs.append(jnp.where(some, top + jnp.log(safe), FAR))
            means.append(jnp.where(some, numer / safe, 0.0))
        own_ref[:, codes] = jnp.concatenate(logs + means, axis=0)
        table = jnp.concatenate(
            [
                pick(first, logs),
                jnp.where(single, FAR, pick(last, logs)),
                pick(first, means),
                jnp.where(single, 0.0, pick(last, means)),
            ],
            axis=0,
        )
        out_ref[:, :, codes] = jnp.broadcast_to(table[None], (out_ref.shape[0], *table.shape))
    marks = jnp.concatenate([first, last, first, last], axis=0).astype(jnp.float32)
    out_ref[:, :, width:] = jnp.broadcast_to(marks[None], (*out_ref.shape[:2], LANES))


def grads_kernel(
    records,
    keys_ref,
    vectors_ref,
    ids_ref,
    own_ref,
    totals_ref,
    leader_ref,
    bias_ref,
    labels_ref,
    grads_ref,
    key_grad_ref,
    held_ref,
    ready_ref,
    sems,
    out_sems,
):
    blocks = fetch(vectors_ref, held_ref, sems)
    keys = keys_ref[...]
    turned = keys.T
    ids = ids_ref[...]
    first, last = ids[:1], ids[-1:]
    masks = [ids == rec for rec in range(records)]
    width = own_ref.shape[1]
    parts = ready_ref.shape[0]
    rows = keys.shape[1] // parts
    widen = lambda lanes: jnp.concatenate([lanes] * (width // LANES), axis=1)
    first_marks = widen(totals_ref[:, 0, width:])
    last_marks = widen(totals_ref[:, 1, width:])
    first_logs, last_logs = totals_ref[:, 0, :width], totals_ref[:, 1, :width]
    first_means, last_means = totals_ref[:, 2, :width], totals_ref[:, 3, :width]
    logs, pools, shows = [], [], []
    for rec in range(records):
        head_logs = jnp.where(first_marks == rec, first_logs, FAR)
        tail_logs = jnp.where(last_marks == rec, last_logs, FAR)
        top = jnp.max(jnp.maximum(head_logs, tail_logs), axis=0, keepdims=True)
        head_weights, tail_weights = jnp.exp(head_logs - top), jnp.exp(tail_logs - top)
        denom = jnp.sum(head_weights + tail_weights, axis=0, keepdims=True)
        numer = jnp.sum(
            head_weights * first_means + tail_weights * last_means, axis=0, keepdims=True
        )
        inner = jnp.logical_and(first < rec, last > rec)
        own_log = own_ref[rec : rec + 1]
        own_mean = own_ref[records + rec : records + rec + 1]
        logs.append(jnp.where(inner, own_log, top + jnp.log(denom)))
        pools.append(jnp.where(inner, own_mean, numer / denom))
        shows.append(jnp.where(inner, 1.0, jnp.where(top > 0.5 * FAR, leader_ref[...], 0.0)))
    logits = jnp.concatenate(pools, axis=0) + bias_ref[...]
    labels_f = labels_ref[...].astype(jnp.float32)
    small = jnp.exp(-jnp.abs(logits))
    loss = jnp.maximum(logits, 0.0) + jnp.log1p(small) - labels_f * logits
    delta = jnp.where(logits >= 0.0, 1.0, small) / (1.0 + small) - labels_f
    show = jnp.concatenate(shows, axis=0) > 0.5
    shown = jnp.concatenate(
        [
            jnp.where(show, loss, 0.0),
            jnp.sum(jnp.where(show, delta, 0.0), axis=0, keepdims=True),
            jnp.zeros((TAIL - records - 1, width), jnp.float32),
        ],
        axis=0,
    )
    ready_ref[:, 2 * rows :, :] = jnp.broadcast_to(shown[None], (parts, *shown.shape))
    deltas = [delta[rec : rec + 1] for rec in range(records)]
    key_grad = jnp.zeros(keys.shape, jnp.float32)
    sent = []
    for codes, copy in blocks:
        copy.wait()
        score_vals, value_vals, query_blk, output_blk = products(keys, held_ref, codes)
        cut = lambda row_list: [row[:, codes] for row in row_list]
        pool_weight = spread(masks, cut(deltas)) * jnp.exp(score_vals - spread(masks, cut(logs)))
        pool_grad = pool_weight.astype(jnp.bfloat16)
        score_grad = (pool_weight * (value_vals - spread(masks, cut(pools)))).astype(jnp.bfloat16)
        ready_ref[:, :rows, codes] = jnp.dot(
            turned, score_grad, preferred_element_type=jnp.float32
        ).reshape(parts, rows, SPAN)
        ready_ref[:, rows : 2 * rows, codes] = jnp.dot(
            turned, pool_grad, preferred_element_type=jnp.float32
        ).reshape(parts, rows, SPAN)
        sent.append(
            pltpu.make_async_copy(
                ready_ref.at[:, :, codes], grads_ref.at[:, :, codes], out_sems.at[len(sent)]
            )
        )
        sent[-1].start()
        key_grad += lax.dot_general(
            score_grad, query_blk, COLS, preferred_element_type=jnp.float32
        )
        key_grad += lax.dot_general(
            pool_grad, output_blk, COLS, preferred_element_type=jnp.float32
        )
    key_grad_ref[...] = key_grad.astype(key_grad_ref.dtype)
    for copy in sent:
        copy.wait()


def pre_grad_kernel(parts_ref, keys_ref, out_ref):
    keys_f = keys_ref[...].astype(jnp.float32)
    total = jnp.sum(parts_ref[...].astype(jnp.float32), axis=0)
    own = (total * (1.0 - keys_f * keys_f)).astype(out_ref.dtype)
    out_ref[...] = jnp.broadcast_to(own[None], out_ref.shape)


def sum_kernel(parts_ref, out_ref):
    own = jnp.sum(parts_ref[...].astype(jnp.float32), axis=0).astype(out_ref.dtype)
    out_ref[...] = jnp.broadcast_to(own[None], out_ref.shape)


def split_kernel(grads_ref, *refs):
    out_refs, sems = refs[:-1], refs[-1]
    copies, row = [], 0
    for out_ref in out_refs:
        rows = out_ref.shape[0]
        copies.append(
            pltpu.make_async_copy(grads_ref.at[row : row + rows], out_ref, sems.at[len(copies)])
        )
        copies[-1].start()
        row += rows
    for copy in copies:
        copy.wait()


def swap(parts, axis):
    return lax.all_to_all(parts, axis, 0, 0, tiled=True)


def struct(shape, dtype):
    return jax.ShapeDtypeStruct(shape, dtype)


def on_device(
    hidden_states, key_weight, queries, output_weight, code_bias, record_ids, code_labels
):
    f32, bf16 = jnp.float32, jnp.bfloat16
    records, width = code_labels.shape
    seq, label = lax.axis_size("seq"), lax.axis_size("label")
    tokens, feats = hidden_states.shape
    dims = key_weight.shape[1]
    rows = queries.shape[0]
    own_toks, own_feats = tokens // label, feats // seq

    few = pltpu.CompilerParams(vmem_limit_bytes=8 * 1024 * 1024)
    many = pltpu.CompilerParams(vmem_limit_bytes=52 * 1024 * 1024)
    most = pltpu.CompilerParams(vmem_limit_bytes=59 * 1024 * 1024)

    vectors = lax.all_gather(jnp.stack([queries, output_weight]), "seq", axis=0)
    partial_pre = jnp.dot(hidden_states, key_weight, preferred_element_type=f32)
    pre_parts = swap(partial_pre.reshape(label, own_toks, dims), "label")
    keys_own = jnp.tanh(jnp.sum(pre_parts, axis=0)).astype(bf16)
    keys_copies = jnp.broadcast_to(keys_own[None], (label, own_toks, dims))
    keys_all = swap(keys_copies, "label").reshape(tokens, dims)

    ids = record_ids[:, None]
    leader = (lax.axis_index("seq") == 0).astype(f32).reshape(1, 1)
    held = pl.BlockSpec(memory_space=pltpu.VMEM)
    far = pl.BlockSpec(memory_space=pltpu.HBM)
    blocks = width // SPAN
    vector_scratch = pltpu.VMEM((seq, 2, rows, width), bf16)
    own_totals, totals = pl.pallas_call(
        lambda *refs: totals_kernel(records, *refs),
        in_specs=[held, far, held],
        out_specs=[held, held],
        out_shape=[
            struct((2 * records, width), f32),
            struct((seq, 4, width + LANES), f32),
        ],
        scratch_shapes=[vector_scratch, pltpu.SemaphoreType.DMA((blocks,))],
        compiler_params=many,
    )(keys_all, vectors, ids)
    totals = swap(totals, "seq")

    grads, key_grad = pl.pallas_call(
        lambda *refs: grads_kernel(records, *refs),
        in_specs=[held, far, *[held] * 6],
        out_specs=[far, held],
        out_shape=[
            struct((seq, 2 * rows + TAIL, width), f32),
            struct((tokens, dims), bf16),
        ],
        scratch_shapes=[
            vector_scratch,
            pltpu.VMEM((seq, 2 * rows + TAIL, width), f32),
            pltpu.SemaphoreType.DMA((blocks,)),
            pltpu.SemaphoreType.DMA((blocks,)),
        ],
        compiler_params=many,
    )(
        keys_all,
        vectors,
        ids,
        own_totals,
        totals,
        leader,
        code_bias[None],
        code_labels,
    )

    grads = lax.psum_scatter(grads, "seq", scatter_dimension=0)
    grad_queries, grad_output, code_loss, grad_bias = pl.pallas_call(
        split_kernel,
        out_shape=[
            struct((rows, width), f32),
            struct((rows, width), f32),
            struct((records, width), f32),
            struct((1, width), f32),
        ],
        in_specs=[far],
        out_specs=[far] * 4,
        scratch_shapes=[pltpu.SemaphoreType.DMA((4,))],
        compiler_params=most,
    )(grads)

    key_parts = swap(key_grad.reshape(label, own_toks, dims), "label")
    pre_copies = pl.pallas_call(
        pre_grad_kernel, out_shape=struct((label, own_toks, dims), bf16), compiler_params=few
    )(key_parts, keys_own)
    pre_grad = swap(pre_copies, "label").reshape(tokens, dims)
    weight_part = lax.dot_general(
        hidden_states, pre_grad, ROWS, preferred_element_type=f32
    ).astype(bf16)
    weight_parts = swap(weight_part.reshape(seq, own_feats, dims), "seq")
    weight_copies = pl.pallas_call(
        sum_kernel, out_shape=struct((seq, own_feats, dims), bf16), compiler_params=few
    )(weight_parts)
    grad_key_weight = swap(weight_copies, "seq").reshape(feats, dims).astype(f32)
    return (code_loss, grad_queries, grad_output, grad_bias[0], grad_key_weight)


def solution(mesh):
    return jax.shard_map(
        on_device,
        mesh=mesh,
        in_specs=(
            P("seq", "label"),
            P("label", None),
            P("seq", "label"),
            P("seq", "label"),
            P("label"),
            P("seq"),
            P(None, "label"),
        ),
        out_specs=(
            P(None, "label"),
            P("seq", "label"),
            P("seq", "label"),
            P("label"),
            P("label", None),
        ),
        check_vma=False,
    )
```

```python
import jax
import jax.numpy as jnp
from jax import lax
from jax.experimental import pallas as pl
from jax.experimental.pallas import tpu as pltpu
from jax.sharding import PartitionSpec as P

FAR = -1e30
ROWS = (((0,), (0,)), ((), ()))
COLS = (((1,), (1,)), ((), ()))
SPAN = 512
LANES = 128


def fetch(vectors_ref, held_ref, sems):
    blocks = []
    for low in range(0, held_ref.shape[-1], SPAN):
        codes = slice(low, low + SPAN)
        copy = pltpu.make_async_copy(
            vectors_ref.at[:, :, :, codes], held_ref.at[:, :, :, codes], sems.at[low // SPAN]
        )
        copy.start()
        blocks.append((codes, copy))
    return blocks


def products(keys, held_ref, codes):
    query_blk = held_ref[:, 0, :, codes].reshape(-1, SPAN)
    output_blk = held_ref[:, 1, :, codes].reshape(-1, SPAN)
    score_vals = jnp.dot(keys, query_blk, preferred_element_type=jnp.float32)
    value_vals = jnp.dot(keys, output_blk, preferred_element_type=jnp.float32)
    return score_vals, value_vals, query_blk, output_blk


def spread(masks, rows):
    spread_vals = rows[-1]
    for mask, row in zip(masks[:-1], rows[:-1]):
        spread_vals = jnp.where(mask, row, spread_vals)
    return spread_vals


def pick(wanted, rows):
    return spread([wanted == rec for rec in range(len(rows))], rows)


def totals_kernel(
    records,
    keys_ref,
    vectors_ref,
    ids_ref,
    own_ref,
    out_ref,
    held_ref,
    sems,
):
    blocks = fetch(vectors_ref, held_ref, sems)
    keys = keys_ref[...]
    ids = ids_ref[...]
    masks = [ids == rec for rec in range(records)]
    first, last = ids[:1], ids[-1:]
    single = first == last
    width = own_ref.shape[1]
    for codes, copy in blocks:
        copy.wait()
        score_vals, value_vals, _, _ = products(keys, held_ref, codes)
        tops = [
            jnp.max(jnp.where(mask, score_vals, FAR), axis=0, keepdims=True) for mask in masks
        ]
        expo = jnp.exp(score_vals - spread(masks, tops))
        weighted = expo * value_vals
        logs, means = [], []
        for mask, top in zip(masks, tops):
            denom = jnp.sum(jnp.where(mask, expo, 0.0), axis=0, keepdims=True)
            numer = jnp.sum(jnp.where(mask, weighted, 0.0), axis=0, keepdims=True)
            some = denom > 0.0
            safe = jnp.where(some, denom, 1.0)
            logs.append(jnp.where(some, top + jnp.log(safe), FAR))
            means.append(jnp.where(some, numer / safe, 0.0))
        own_ref[:, codes] = jnp.concatenate(logs + means, axis=0)
        table = jnp.concatenate(
            [
                pick(first, logs),
                jnp.where(single, FAR, pick(last, logs)),
                pick(first, means),
                jnp.where(single, 0.0, pick(last, means)),
            ],
            axis=0,
        )
        out_ref[:, :, codes] = jnp.broadcast_to(table[None], (out_ref.shape[0], *table.shape))
    marks = jnp.concatenate([first, last, first, last], axis=0).astype(jnp.float32)
    out_ref[:, :, width:] = jnp.broadcast_to(marks[None], (*out_ref.shape[:2], LANES))


def halves(vals):
    high = vals.astype(jnp.bfloat16).astype(jnp.float32)
    return high, vals - high


def grads_kernel(
    records,
    keys_ref,
    vectors_ref,
    ids_ref,
    own_ref,
    totals_ref,
    leader_ref,
    bias_ref,
    labels_ref,
    grads_ref,
    key_grad_ref,
    held_ref,
    ready_ref,
    sems,
    out_sems,
):
    blocks = fetch(vectors_ref, held_ref, sems)
    keys = keys_ref[...]
    turned = keys.T
    ids = ids_ref[...]
    first, last = ids[:1], ids[-1:]
    masks = [ids == rec for rec in range(records)]
    width = own_ref.shape[1]
    parts = ready_ref.shape[0]
    rows = keys.shape[1] // parts
    widen = lambda lanes: jnp.concatenate([lanes] * (width // LANES), axis=1)
    first_marks = widen(totals_ref[:, 0, width:])
    last_marks = widen(totals_ref[:, 1, width:])
    first_logs, last_logs = totals_ref[:, 0, :width], totals_ref[:, 1, :width]
    first_means, last_means = totals_ref[:, 2, :width], totals_ref[:, 3, :width]
    logs, pools, shows = [], [], []
    for rec in range(records):
        head_logs = jnp.where(first_marks == rec, first_logs, FAR)
        tail_logs = jnp.where(last_marks == rec, last_logs, FAR)
        top = jnp.max(jnp.maximum(head_logs, tail_logs), axis=0, keepdims=True)
        head_weights, tail_weights = jnp.exp(head_logs - top), jnp.exp(tail_logs - top)
        denom = jnp.sum(head_weights + tail_weights, axis=0, keepdims=True)
        numer = jnp.sum(
            head_weights * first_means + tail_weights * last_means, axis=0, keepdims=True
        )
        inner = jnp.logical_and(first < rec, last > rec)
        own_log = own_ref[rec : rec + 1]
        own_mean = own_ref[records + rec : records + rec + 1]
        logs.append(jnp.where(inner, own_log, top + jnp.log(denom)))
        pools.append(jnp.where(inner, own_mean, numer / denom))
        shows.append(jnp.where(inner, 1.0, jnp.where(top > 0.5 * FAR, leader_ref[...], 0.0)))
    logits = jnp.concatenate(pools, axis=0) + bias_ref[...]
    labels_f = labels_ref[...].astype(jnp.float32)
    small = jnp.exp(-jnp.abs(logits))
    loss = jnp.maximum(logits, 0.0) + jnp.log1p(small) - labels_f * logits
    delta = jnp.where(logits >= 0.0, 1.0, small) / (1.0 + small) - labels_f
    show = jnp.concatenate(shows, axis=0) > 0.5
    shown = [*halves(jnp.where(show, loss, 0.0)), *halves(jnp.where(show, delta, 0.0))]
    shown = jnp.concatenate(shown, axis=0).astype(ready_ref.dtype)
    ready_ref[:, 2 * rows :, :] = jnp.broadcast_to(shown[None], (parts, *shown.shape))
    deltas = [delta[rec : rec + 1] for rec in range(records)]
    key_grad = jnp.zeros(keys.shape, jnp.float32)
    sent = []
    for codes, copy in blocks:
        copy.wait()
        score_vals, value_vals, query_blk, output_blk = products(keys, held_ref, codes)
        cut = lambda row_list: [row[:, codes] for row in row_list]
        pool_weight = spread(masks, cut(deltas)) * jnp.exp(score_vals - spread(masks, cut(logs)))
        pool_grad = pool_weight.astype(jnp.bfloat16)
        score_grad = (pool_weight * (value_vals - spread(masks, cut(pools)))).astype(jnp.bfloat16)
        for half, grad in enumerate((score_grad, pool_grad)):
            sums = jnp.dot(turned, grad, preferred_element_type=jnp.float32)
            ready_ref[:, half * rows : (half + 1) * rows, codes] = sums.astype(
                ready_ref.dtype
            ).reshape(parts, rows, SPAN)
        sent.append(
            pltpu.make_async_copy(
                ready_ref.at[:, :, codes], grads_ref.at[:, :, codes], out_sems.at[len(sent)]
            )
        )
        sent[-1].start()
        key_grad += lax.dot_general(
            score_grad, query_blk, COLS, preferred_element_type=jnp.float32
        )
        key_grad += lax.dot_general(
            pool_grad, output_blk, COLS, preferred_element_type=jnp.float32
        )
    key_grad_ref[...] = key_grad.astype(key_grad_ref.dtype)
    for copy in sent:
        copy.wait()


def pre_grad_kernel(parts_ref, keys_ref, out_ref):
    keys_f = keys_ref[...].astype(jnp.float32)
    total = jnp.sum(parts_ref[...].astype(jnp.float32), axis=0)
    own = (total * (1.0 - keys_f * keys_f)).astype(out_ref.dtype)
    out_ref[...] = jnp.broadcast_to(own[None], out_ref.shape)


def sum_kernel(parts_ref, out_ref):
    own = jnp.sum(parts_ref[...].astype(jnp.float32), axis=0).astype(out_ref.dtype)
    out_ref[...] = jnp.broadcast_to(own[None], out_ref.shape)


def final_kernel(
    grads_ref, weight_ref, loss_ref, grad_query_ref, grad_output_ref, grad_bias_ref, out_ref
):
    rows, records = grad_query_ref.shape[0], loss_ref.shape[0]
    grad_query_ref[...] = grads_ref[:rows].astype(jnp.float32)
    grad_output_ref[...] = grads_ref[rows : 2 * rows].astype(jnp.float32)
    shown = grads_ref[2 * rows :].astype(jnp.float32)
    loss_ref[...] = shown[:records] + shown[records : 2 * records]
    grad_bias_ref[...] = jnp.sum(shown[2 * records :], axis=0, keepdims=True)
    out_ref[...] = weight_ref[...].astype(jnp.float32)


def swap(parts, axis):
    return lax.all_to_all(parts, axis, 0, 0, tiled=True)


def struct(shape, dtype):
    return jax.ShapeDtypeStruct(shape, dtype)


def on_device(
    hidden_states, key_weight, queries, output_weight, code_bias, record_ids, code_labels
):
    f32, bf16 = jnp.float32, jnp.bfloat16
    records, width = code_labels.shape
    seq, label = lax.axis_size("seq"), lax.axis_size("label")
    tokens, feats = hidden_states.shape
    dims = key_weight.shape[1]
    rows = queries.shape[0]
    own_toks, own_feats = tokens // label, feats // seq

    few = pltpu.CompilerParams(vmem_limit_bytes=8 * 1024 * 1024)
    many = pltpu.CompilerParams(vmem_limit_bytes=52 * 1024 * 1024)

    vectors = lax.all_gather(jnp.stack([queries, output_weight]), "seq", axis=0)
    partial_pre = jnp.dot(hidden_states, key_weight, preferred_element_type=f32)
    pre_parts = swap(partial_pre.reshape(label, own_toks, dims), "label")
    keys_own = jnp.tanh(jnp.sum(pre_parts, axis=0)).astype(bf16)
    keys_copies = jnp.broadcast_to(keys_own[None], (label, own_toks, dims))
    keys_all = swap(keys_copies, "label").reshape(tokens, dims)

    ids = record_ids[:, None]
    leader = (lax.axis_index("seq") == 0).astype(f32).reshape(1, 1)
    held = pl.BlockSpec(memory_space=pltpu.VMEM)
    far = pl.BlockSpec(memory_space=pltpu.HBM)
    blocks = width // SPAN
    vector_scratch = pltpu.VMEM((seq, 2, rows, width), bf16)
    own_totals, totals = pl.pallas_call(
        lambda *refs: totals_kernel(records, *refs),
        in_specs=[held, far, held],
        out_specs=[held, held],
        out_shape=[
            struct((2 * records, width), f32),
            struct((seq, 4, width + LANES), f32),
        ],
        scratch_shapes=[vector_scratch, pltpu.SemaphoreType.DMA((blocks,))],
        compiler_params=many,
    )(keys_all, vectors, ids)
    totals = swap(totals, "seq")

    grads, key_grad = pl.pallas_call(
        lambda *refs: grads_kernel(records, *refs),
        in_specs=[held, far, *[held] * 6],
        out_specs=[far, held],
        out_shape=[
            struct((seq, 2 * rows + 4 * records, width), bf16),
            struct((tokens, dims), bf16),
        ],
        scratch_shapes=[
            vector_scratch,
            pltpu.VMEM((seq, 2 * rows + 4 * records, width), bf16),
            pltpu.SemaphoreType.DMA((blocks,)),
            pltpu.SemaphoreType.DMA((blocks,)),
        ],
        compiler_params=many,
    )(
        keys_all,
        vectors,
        ids,
        own_totals,
        totals,
        leader,
        code_bias[None],
        code_labels,
    )

    grads = lax.psum_scatter(grads, "seq", scatter_dimension=0)

    key_parts = swap(key_grad.reshape(label, own_toks, dims), "label")
    pre_copies = pl.pallas_call(
        pre_grad_kernel, out_shape=struct((label, own_toks, dims), bf16), compiler_params=few
    )(key_parts, keys_own)
    pre_grad = swap(pre_copies, "label").reshape(tokens, dims)
    weight_part = lax.dot_general(
        hidden_states, pre_grad, ROWS, preferred_element_type=f32
    ).astype(bf16)
    weight_parts = swap(weight_part.reshape(seq, own_feats, dims), "seq")
    weight_copies = pl.pallas_call(
        sum_kernel, out_shape=struct((seq, own_feats, dims), bf16), compiler_params=few
    )(weight_parts)
    weights = swap(weight_copies, "seq").reshape(feats, dims)
    code_loss, grad_queries, grad_output, grad_bias, grad_key_weight = pl.pallas_call(
        final_kernel,
        out_shape=[
            struct((records, width), f32),
            struct((rows, width), f32),
            struct((rows, width), f32),
            struct((1, width), f32),
            struct((feats, dims), f32),
        ],
        in_specs=[held, held],
        out_specs=[held] * 5,
        compiler_params=many,
    )(grads, weights)
    return (code_loss, grad_queries, grad_output, grad_bias[0], grad_key_weight)


def solution(mesh):
    return jax.shard_map(
        on_device,
        mesh=mesh,
        in_specs=(
            P("seq", "label"),
            P("label", None),
            P("seq", "label"),
            P("seq", "label"),
            P("label"),
            P("seq"),
            P(None, "label"),
        ),
        out_specs=(
            P(None, "label"),
            P("seq", "label"),
            P("seq", "label"),
            P("label"),
            P("label", None),
        ),
        check_vma=False,
    )
```

```python
import jax
import jax.numpy as jnp
from jax import lax
from jax.experimental import pallas as pl
from jax.experimental.pallas import tpu as pltpu
from jax.sharding import PartitionSpec as P

FAR = -1e30
ROWS = (((0,), (0,)), ((), ()))
COLS = (((1,), (1,)), ((), ()))
SPAN = 512
LANES = 128
FOUR = 4


def pack_kernel(query_ref, output_ref, hidden_ref, out_ref):
    out_ref[0] = query_ref[...]
    out_ref[1] = output_ref[...]
    rows = out_ref.shape[1]
    quarter = hidden_ref.shape[0] // FOUR
    low = 0
    for half in range(quarter // rows):
        for four in range(FOUR):
            first = four * quarter + half * rows
            out_ref[2, :, low : low + LANES] = hidden_ref[first : first + rows]
            low += LANES


def fetch(vectors_ref, held_ref, sems):
    blocks = []
    for low in range(0, held_ref.shape[-1], SPAN):
        codes = slice(low, low + SPAN)
        copy = pltpu.make_async_copy(
            vectors_ref.at[:, :2, :, codes], held_ref.at[:, :, :, codes], sems.at[low // SPAN]
        )
        copy.start()
        blocks.append((codes, copy))
    return blocks


def products(keys, held_ref, codes):
    query_blk = held_ref[:, 0, :, codes].reshape(-1, SPAN)
    output_blk = held_ref[:, 1, :, codes].reshape(-1, SPAN)
    score_vals = jnp.dot(keys, query_blk, preferred_element_type=jnp.float32)
    value_vals = jnp.dot(keys, output_blk, preferred_element_type=jnp.float32)
    return score_vals, value_vals, query_blk, output_blk


def spread(masks, rows):
    spread_vals = rows[-1]
    for mask, row in zip(masks[:-1], rows[:-1]):
        spread_vals = jnp.where(mask, row, spread_vals)
    return spread_vals


def pick(wanted, rows):
    return spread([wanted == rec for rec in range(len(rows))], rows)


def totals_kernel(
    records,
    keys_ref,
    vectors_ref,
    ids_ref,
    own_ref,
    out_ref,
    held_ref,
    sems,
):
    blocks = fetch(vectors_ref, held_ref, sems)
    keys = keys_ref[...]
    ids = ids_ref[...]
    masks = [ids == rec for rec in range(records)]
    first = jnp.min(ids, axis=0, keepdims=True)
    last = jnp.max(ids, axis=0, keepdims=True)
    single = first == last
    width = own_ref.shape[1]
    for codes, copy in blocks:
        copy.wait()
        score_vals, value_vals, _, _ = products(keys, held_ref, codes)
        tops = [
            jnp.max(jnp.where(mask, score_vals, FAR), axis=0, keepdims=True) for mask in masks
        ]
        expo = jnp.exp(score_vals - spread(masks, tops))
        weighted = expo * value_vals
        logs, means = [], []
        for mask, top in zip(masks, tops):
            denom = jnp.sum(jnp.where(mask, expo, 0.0), axis=0, keepdims=True)
            numer = jnp.sum(jnp.where(mask, weighted, 0.0), axis=0, keepdims=True)
            some = denom > 0.0
            safe = jnp.where(some, denom, 1.0)
            logs.append(jnp.where(some, top + jnp.log(safe), FAR))
            means.append(jnp.where(some, numer / safe, 0.0))
        own_ref[:, codes] = jnp.concatenate(logs + means, axis=0)
        table = jnp.concatenate(
            [
                pick(first, logs),
                jnp.where(single, FAR, pick(last, logs)),
                pick(first, means),
                jnp.where(single, 0.0, pick(last, means)),
            ],
            axis=0,
        )
        out_ref[:, :, codes] = jnp.broadcast_to(table[None], (out_ref.shape[0], *table.shape))
    marks = jnp.concatenate([first, last, first, last], axis=0).astype(jnp.float32)
    out_ref[:, :, width:] = jnp.broadcast_to(marks[None], (*out_ref.shape[:2], LANES))


def halves(vals):
    high = vals.astype(jnp.bfloat16).astype(jnp.float32)
    return high, vals - high


def grads_kernel(
    records,
    keys_ref,
    vectors_ref,
    ids_ref,
    own_ref,
    totals_ref,
    leader_ref,
    bias_ref,
    labels_ref,
    grads_ref,
    key_grad_ref,
    held_ref,
    ready_ref,
    sems,
    out_sems,
):
    blocks = fetch(vectors_ref, held_ref, sems)
    keys = keys_ref[...]
    turned = keys.T
    ids = ids_ref[...]
    first = jnp.min(ids, axis=0, keepdims=True)
    last = jnp.max(ids, axis=0, keepdims=True)
    masks = [ids == rec for rec in range(records)]
    width = own_ref.shape[1]
    parts = ready_ref.shape[0]
    rows = keys.shape[1] // parts
    widen = lambda lanes: jnp.concatenate([lanes] * (width // LANES), axis=1)
    first_marks = widen(totals_ref[:, 0, width:])
    last_marks = widen(totals_ref[:, 1, width:])
    first_logs, last_logs = totals_ref[:, 0, :width], totals_ref[:, 1, :width]
    first_means, last_means = totals_ref[:, 2, :width], totals_ref[:, 3, :width]
    logs, pools, shows = [], [], []
    for rec in range(records):
        head_logs = jnp.where(first_marks == rec, first_logs, FAR)
        tail_logs = jnp.where(last_marks == rec, last_logs, FAR)
        top = jnp.max(jnp.maximum(head_logs, tail_logs), axis=0, keepdims=True)
        head_weights, tail_weights = jnp.exp(head_logs - top), jnp.exp(tail_logs - top)
        denom = jnp.sum(head_weights + tail_weights, axis=0, keepdims=True)
        numer = jnp.sum(
            head_weights * first_means + tail_weights * last_means, axis=0, keepdims=True
        )
        inner = jnp.logical_and(first < rec, last > rec)
        own_log = own_ref[rec : rec + 1]
        own_mean = own_ref[records + rec : records + rec + 1]
        logs.append(jnp.where(inner, own_log, top + jnp.log(denom)))
        pools.append(jnp.where(inner, own_mean, numer / denom))
        shows.append(jnp.where(inner, 1.0, jnp.where(top > 0.5 * FAR, leader_ref[...], 0.0)))
    logits = jnp.concatenate(pools, axis=0) + bias_ref[...]
    labels_f = labels_ref[...].astype(jnp.float32)
    small = jnp.exp(-jnp.abs(logits))
    loss = jnp.maximum(logits, 0.0) + jnp.log1p(small) - labels_f * logits
    delta = jnp.where(logits >= 0.0, 1.0, small) / (1.0 + small) - labels_f
    show = jnp.concatenate(shows, axis=0) > 0.5
    shown = [*halves(jnp.where(show, loss, 0.0)), *halves(jnp.where(show, delta, 0.0))]
    shown = jnp.concatenate(shown, axis=0).astype(ready_ref.dtype)
    ready_ref[:, 2 * rows :, :] = jnp.broadcast_to(shown[None], (parts, *shown.shape))
    deltas = [delta[rec : rec + 1] for rec in range(records)]
    key_grad = jnp.zeros(keys.shape, jnp.float32)
    sent = []
    for codes, copy in blocks:
        copy.wait()
        score_vals, value_vals, query_blk, output_blk = products(keys, held_ref, codes)
        cut = lambda row_list: [row[:, codes] for row in row_list]
        pool_weight = spread(masks, cut(deltas)) * jnp.exp(score_vals - spread(masks, cut(logs)))
        pool_grad = pool_weight.astype(jnp.bfloat16)
        score_grad = (pool_weight * (value_vals - spread(masks, cut(pools)))).astype(jnp.bfloat16)
        for half, grad in enumerate((score_grad, pool_grad)):
            sums = jnp.dot(turned, grad, preferred_element_type=jnp.float32)
            ready_ref[:, half * rows : (half + 1) * rows, codes] = sums.astype(
                ready_ref.dtype
            ).reshape(parts, rows, SPAN)
        sent.append(
            pltpu.make_async_copy(
                ready_ref.at[:, :, codes], grads_ref.at[:, :, codes], out_sems.at[len(sent)]
            )
        )
        sent[-1].start()
        key_grad += lax.dot_general(
            score_grad, query_blk, COLS, preferred_element_type=jnp.float32
        )
        key_grad += lax.dot_general(
            pool_grad, output_blk, COLS, preferred_element_type=jnp.float32
        )
    key_grad_ref[...] = key_grad.astype(key_grad_ref.dtype)
    for copy in sent:
        copy.wait()


def pre_grad_kernel(parts_ref, keys_ref, out_ref):
    keys_f = keys_ref[...].astype(jnp.float32)
    total = jnp.sum(parts_ref[...].astype(jnp.float32), axis=0)
    own = total * (1.0 - keys_f * keys_f)
    toks = own.shape[0]
    cols = LANES // FOUR
    receivers = own.shape[1] // cols
    copies = out_ref.shape[0] // receivers // toks
    place = lax.broadcasted_iota(jnp.int32, (toks, LANES), 1) // cols
    token = lax.broadcasted_iota(jnp.int32, (toks, LANES), 0) // (toks // FOUR)
    row = 0
    for low in range(0, own.shape[1], LANES):
        tile = own[:, low : low + LANES]
        turns = [tile] + [pltpu.roll(tile, cols * turn, 1) for turn in range(1, FOUR)]
        for group in range(FOUR):
            side = jnp.zeros_like(tile)
            for spot in range(FOUR):
                here = jnp.logical_and(place == spot, token == spot)
                side = jnp.where(here, turns[(spot - group) % FOUR], side)
            step = toks // FOUR
            side = side + pltpu.roll(side, step, 0)
            side = side + pltpu.roll(side, 2 * step, 0)
            block = jnp.concatenate([side] * copies, axis=0).astype(out_ref.dtype)
            out_ref[row : row + block.shape[0]] = block
            row += block.shape[0]


def weight_kernel(parts_ref, vectors_ref, out_ref, hidden_ref, sem):
    copy = pltpu.make_async_copy(vectors_ref.at[:, 2], hidden_ref, sem)
    copy.start()
    seq, rows, width = hidden_ref.shape
    parts = parts_ref[...].reshape(seq, -1, LANES)
    copy.wait()
    lanes = FOUR * LANES
    total = jnp.zeros((LANES, lanes), jnp.float32)
    for half in range(width // lanes):
        total += lax.dot_general(
            parts[:, half * rows : (half + 1) * rows].reshape(-1, LANES),
            hidden_ref[:, :, half * lanes : (half + 1) * lanes].reshape(-1, lanes),
            ROWS,
            preferred_element_type=jnp.float32,
        )
    cols = LANES // FOUR
    own = jnp.zeros((cols, LANES), jnp.float32)
    for spot in range(FOUR):
        own += total[spot * cols : (spot + 1) * cols, spot * LANES : (spot + 1) * LANES]
    out_ref[...] = jnp.broadcast_to(own.astype(out_ref.dtype)[None], out_ref.shape)


def final_kernel(
    grads_ref, weight_ref, loss_ref, grad_query_ref, grad_output_ref, grad_bias_ref, out_ref
):
    rows, records = grad_query_ref.shape[0], loss_ref.shape[0]
    grad_query_ref[...] = grads_ref[:rows].astype(jnp.float32)
    grad_output_ref[...] = grads_ref[rows : 2 * rows].astype(jnp.float32)
    shown = grads_ref[2 * rows :].astype(jnp.float32)
    loss_ref[...] = shown[:records] + shown[records : 2 * records]
    grad_bias_ref[...] = jnp.sum(shown[2 * records :], axis=0, keepdims=True)
    out_ref[...] = weight_ref[...].astype(jnp.float32).T


def swap(parts, axis):
    return lax.all_to_all(parts, axis, 0, 0, tiled=True)


def struct(shape, dtype):
    return jax.ShapeDtypeStruct(shape, dtype)


def on_device(
    hidden_states, key_weight, queries, output_weight, code_bias, record_ids, code_labels
):
    f32, bf16 = jnp.float32, jnp.bfloat16
    records, width = code_labels.shape
    seq, label = lax.axis_size("seq"), lax.axis_size("label")
    tokens, feats = hidden_states.shape
    dims = key_weight.shape[1]
    rows = queries.shape[0]
    own_toks = tokens // label

    few = pltpu.CompilerParams(vmem_limit_bytes=8 * 1024 * 1024)
    many = pltpu.CompilerParams(vmem_limit_bytes=52 * 1024 * 1024)

    quarters = hidden_states.reshape(FOUR, label, -1, feats)
    ordered = quarters.transpose(1, 0, 2, 3).reshape(tokens, feats)
    ids = record_ids.reshape(FOUR, label, -1).transpose(1, 0, 2).reshape(tokens, 1)
    vectors = pl.pallas_call(
        pack_kernel,
        out_shape=struct((3, rows, width), bf16),
        compiler_params=pltpu.CompilerParams(vmem_limit_bytes=59 * 1024 * 1024),
    )(queries, output_weight, hidden_states)
    vectors = lax.all_gather(vectors, "seq", axis=0)
    partial_pre = jnp.dot(ordered, key_weight, preferred_element_type=f32)
    pre_parts = swap(partial_pre.reshape(label, own_toks, dims), "label")
    keys_own = jnp.tanh(jnp.sum(pre_parts, axis=0)).astype(bf16)
    keys_copies = jnp.broadcast_to(keys_own[None], (label, own_toks, dims))
    keys_all = swap(keys_copies, "label").reshape(tokens, dims)

    leader = (lax.axis_index("seq") == 0).astype(f32).reshape(1, 1)
    held = pl.BlockSpec(memory_space=pltpu.VMEM)
    far = pl.BlockSpec(memory_space=pltpu.HBM)
    blocks = width // SPAN
    vector_scratch = pltpu.VMEM((seq, 2, rows, width), bf16)
    own_totals, totals = pl.pallas_call(
        lambda *refs: totals_kernel(records, *refs),
        in_specs=[held, far, held],
        out_specs=[held, held],
        out_shape=[
            struct((2 * records, width), f32),
            struct((seq, 4, width + LANES), f32),
        ],
        scratch_shapes=[vector_scratch, pltpu.SemaphoreType.DMA((blocks,))],
        compiler_params=many,
    )(keys_all, vectors, ids)
    totals = swap(totals, "seq")

    grads, key_grad = pl.pallas_call(
        lambda *refs: grads_kernel(records, *refs),
        in_specs=[held, far, *[held] * 6],
        out_specs=[far, held],
        out_shape=[
            struct((seq, 2 * rows + 4 * records, width), bf16),
            struct((tokens, dims), bf16),
        ],
        scratch_shapes=[
            vector_scratch,
            pltpu.VMEM((seq, 2 * rows + 4 * records, width), bf16),
            pltpu.SemaphoreType.DMA((blocks,)),
            pltpu.SemaphoreType.DMA((blocks,)),
        ],
        compiler_params=many,
    )(
        keys_all,
        vectors,
        ids,
        own_totals,
        totals,
        leader,
        code_bias[None],
        code_labels,
    )

    grads = lax.psum_scatter(grads, "seq", scatter_dimension=0)

    key_parts = swap(key_grad.reshape(label, own_toks, dims), "label")
    pre_parts = pl.pallas_call(
        pre_grad_kernel, out_shape=struct((tokens * seq // FOUR, LANES), bf16), compiler_params=few
    )(key_parts, keys_own)
    pre_parts = swap(pre_parts, ("seq", "label"))
    weight_copies = pl.pallas_call(
        weight_kernel,
        in_specs=[held, far],
        out_specs=held,
        out_shape=struct((seq, dims // seq, feats), bf16),
        scratch_shapes=[
            pltpu.VMEM((seq, rows, width), bf16),
            pltpu.SemaphoreType.DMA(()),
        ],
        compiler_params=many,
    )(pre_parts, vectors)
    weights = swap(weight_copies, "seq").reshape(dims, feats)
    code_loss, grad_queries, grad_output, grad_bias, grad_key_weight = pl.pallas_call(
        final_kernel,
        out_shape=[
            struct((records, width), f32),
            struct((rows, width), f32),
            struct((rows, width), f32),
            struct((1, width), f32),
            struct((feats, dims), f32),
        ],
        in_specs=[held, held],
        out_specs=[held] * 5,
        compiler_params=many,
    )(grads, weights)
    return (code_loss, grad_queries, grad_output, grad_bias[0], grad_key_weight)


def solution(mesh):
    return jax.shard_map(
        on_device,
        mesh=mesh,
        in_specs=(
            P("seq", "label"),
            P("label", None),
            P("seq", "label"),
            P("seq", "label"),
            P("label"),
            P("seq"),
            P(None, "label"),
        ),
        out_specs=(
            P(None, "label"),
            P("seq", "label"),
            P("seq", "label"),
            P("label"),
            P("label", None),
        ),
        check_vma=False,
    )
```

```python
import jax
import jax.numpy as jnp
from jax import lax
from jax.experimental import pallas as pl
from jax.experimental.pallas import tpu as pltpu
from jax.sharding import PartitionSpec as P

FAR = -1e30
ROWS = (((0,), (0,)), ((), ()))
COLS = (((1,), (1,)), ((), ()))
SPAN = 512
LANES = 128


def fetch(vectors_ref, held_ref, sems):
    blocks = []
    for low in range(0, held_ref.shape[-1], SPAN):
        codes = slice(low, low + SPAN)
        copy = pltpu.make_async_copy(
            vectors_ref.at[:, :, :, codes], held_ref.at[:, :, :, codes], sems.at[low // SPAN]
        )
        copy.start()
        blocks.append((codes, copy))
    return blocks


def products(keys, held_ref, codes):
    query_blk = held_ref[:, 0, :, codes].reshape(-1, SPAN)
    output_blk = held_ref[:, 1, :, codes].reshape(-1, SPAN)
    score_vals = jnp.dot(keys, query_blk, preferred_element_type=jnp.float32)
    value_vals = jnp.dot(keys, output_blk, preferred_element_type=jnp.float32)
    return score_vals, value_vals, query_blk, output_blk


def spread(masks, rows):
    spread_vals = rows[-1]
    for mask, row in zip(masks[:-1], rows[:-1]):
        spread_vals = jnp.where(mask, row, spread_vals)
    return spread_vals


def totals_kernel(
    records, keys_ref, vectors_ref, ids_ref, own_ref, out_ref, held_ref, sems
):
    blocks = fetch(vectors_ref, held_ref, sems)
    keys = keys_ref[...]
    ids = ids_ref[...]
    first, last = ids[:1], ids[-1:]
    single = first == last
    between = jnp.max(last - first) > 1
    heads, tails = ids == first, ids == last
    width = own_ref.shape[1]

    def totals(top, expo, weighted):
        denom = jnp.sum(expo, axis=0, keepdims=True)
        numer = jnp.sum(weighted, axis=0, keepdims=True)
        some = denom > 0.0
        safe = jnp.where(some, denom, 1.0)
        return jnp.where(some, top + jnp.log(safe), FAR), jnp.where(some, numer / safe, 0.0)

    for codes, copy in blocks:
        copy.wait()
        score_vals, value_vals, _, _ = products(keys, held_ref, codes)
        head_top = jnp.max(jnp.where(heads, score_vals, FAR), axis=0, keepdims=True)
        tail_top = jnp.max(jnp.where(tails, score_vals, FAR), axis=0, keepdims=True)
        shifted = jnp.where(heads, score_vals - head_top, score_vals - tail_top)
        expo = jnp.exp(jnp.where(jnp.logical_or(heads, tails), shifted, FAR))
        weighted = expo * value_vals
        head_expo = jnp.where(heads, expo, 0.0)
        head_weighted = jnp.where(heads, weighted, 0.0)
        head_log, head_mean = totals(head_top, head_expo, head_weighted)
        tail_log, tail_mean = totals(tail_top, expo - head_expo, weighted - head_weighted)
        table = jnp.concatenate(
            [
                head_log,
                jnp.where(single, FAR, tail_log),
                head_mean,
                jnp.where(single, 0.0, tail_mean),
            ],
            axis=0,
        )
        out_ref[:, :, codes] = jnp.broadcast_to(table[None], (out_ref.shape[0], *table.shape))

        @pl.when(between)
        def _():
            for rec in range(records):
                mask = ids == rec
                top = jnp.max(jnp.where(mask, score_vals, FAR), axis=0, keepdims=True)
                inner = jnp.where(mask, jnp.exp(jnp.where(mask, score_vals - top, FAR)), 0.0)
                log, mean = totals(top, inner, inner * value_vals)
                own_ref[rec : rec + 1, codes] = log
                own_ref[records + rec : records + rec + 1, codes] = mean

    marks = jnp.concatenate([first, last, first, last], axis=0).astype(jnp.float32)
    out_ref[:, :, width:] = jnp.broadcast_to(marks[None], (*out_ref.shape[:2], LANES))


def halves(vals):
    high = vals.astype(jnp.bfloat16).astype(jnp.float32)
    return high, vals - high


def grads_kernel(
    records,
    keys_ref,
    vectors_ref,
    ids_ref,
    own_ref,
    totals_ref,
    leader_ref,
    bias_ref,
    labels_ref,
    grads_ref,
    key_grad_ref,
    held_ref,
    ready_ref,
    sems,
    out_sems,
):
    blocks = fetch(vectors_ref, held_ref, sems)
    keys = keys_ref[...]
    turned = keys.T
    ids = ids_ref[...]
    first, last = ids[:1], ids[-1:]
    masks = [ids == rec for rec in range(records)]
    width = own_ref.shape[1]
    parts = ready_ref.shape[0]
    rows = keys.shape[1] // parts
    widen = lambda lanes: jnp.concatenate([lanes] * (width // LANES), axis=1)
    first_marks = widen(totals_ref[:, 0, width:])
    last_marks = widen(totals_ref[:, 1, width:])
    first_logs, last_logs = totals_ref[:, 0, :width], totals_ref[:, 1, :width]
    first_means, last_means = totals_ref[:, 2, :width], totals_ref[:, 3, :width]
    logs, pools, shows = [], [], []
    for rec in range(records):
        head_logs = jnp.where(first_marks == rec, first_logs, FAR)
        tail_logs = jnp.where(last_marks == rec, last_logs, FAR)
        top = jnp.max(jnp.maximum(head_logs, tail_logs), axis=0, keepdims=True)
        head_weights, tail_weights = jnp.exp(head_logs - top), jnp.exp(tail_logs - top)
        denom = jnp.sum(head_weights + tail_weights, axis=0, keepdims=True)
        numer = jnp.sum(
            head_weights * first_means + tail_weights * last_means, axis=0, keepdims=True
        )
        inner = jnp.logical_and(first < rec, last > rec)
        own_log = own_ref[rec : rec + 1]
        own_mean = own_ref[records + rec : records + rec + 1]
        logs.append(jnp.where(inner, own_log, top + jnp.log(denom)))
        pools.append(jnp.where(inner, own_mean, numer / denom))
        shows.append(jnp.where(inner, 1.0, jnp.where(top > 0.5 * FAR, leader_ref[...], 0.0)))
    logits = jnp.concatenate(pools, axis=0) + bias_ref[...]
    labels_f = labels_ref[...].astype(jnp.float32)
    small = jnp.exp(-jnp.abs(logits))
    loss = jnp.maximum(logits, 0.0) + jnp.log1p(small) - labels_f * logits
    delta = jnp.where(logits >= 0.0, 1.0, small) / (1.0 + small) - labels_f
    show = jnp.concatenate(shows, axis=0) > 0.5
    shown = [*halves(jnp.where(show, loss, 0.0)), *halves(jnp.where(show, delta, 0.0))]
    shown = jnp.concatenate(shown, axis=0).astype(ready_ref.dtype)
    ready_ref[:, 2 * rows :, :] = jnp.broadcast_to(shown[None], (parts, *shown.shape))
    deltas = [delta[rec : rec + 1] for rec in range(records)]
    key_grad = jnp.zeros(keys.shape, jnp.float32)
    sent = []
    for codes, copy in blocks:
        copy.wait()
        score_vals, value_vals, query_blk, output_blk = products(keys, held_ref, codes)
        cut = lambda row_list: [row[:, codes] for row in row_list]
        pool_weight = spread(masks, cut(deltas)) * jnp.exp(score_vals - spread(masks, cut(logs)))
        pool_grad = pool_weight.astype(jnp.bfloat16)
        score_grad = (pool_weight * (value_vals - spread(masks, cut(pools)))).astype(jnp.bfloat16)
        for half, grad in enumerate((score_grad, pool_grad)):
            sums = jnp.dot(turned, grad, preferred_element_type=jnp.float32)
            ready_ref[:, half * rows : (half + 1) * rows, codes] = sums.astype(
                ready_ref.dtype
            ).reshape(parts, rows, SPAN)
        sent.append(
            pltpu.make_async_copy(
                ready_ref.at[:, :, codes], grads_ref.at[:, :, codes], out_sems.at[len(sent)]
            )
        )
        sent[-1].start()
        key_grad += lax.dot_general(
            score_grad, query_blk, COLS, preferred_element_type=jnp.float32
        )
        key_grad += lax.dot_general(
            pool_grad, output_blk, COLS, preferred_element_type=jnp.float32
        )
    key_grad_ref[...] = key_grad.astype(key_grad_ref.dtype)
    for copy in sent:
        copy.wait()


def pre_grad_kernel(parts_ref, keys_ref, out_ref):
    keys_f = keys_ref[...].astype(jnp.float32)
    total = jnp.sum(parts_ref[...].astype(jnp.float32), axis=0)
    own = (total * (1.0 - keys_f * keys_f)).astype(out_ref.dtype)
    out_ref[...] = jnp.broadcast_to(own[None], out_ref.shape)


def sum_kernel(parts_ref, out_ref):
    own = jnp.sum(parts_ref[...].astype(jnp.float32), axis=0).astype(out_ref.dtype)
    out_ref[...] = jnp.broadcast_to(own[None], out_ref.shape)


def final_kernel(
    grads_ref, weight_ref, loss_ref, grad_query_ref, grad_output_ref, grad_bias_ref, out_ref
):
    rows, records = grad_query_ref.shape[0], loss_ref.shape[0]
    grad_query_ref[...] = grads_ref[:rows].astype(jnp.float32)
    grad_output_ref[...] = grads_ref[rows : 2 * rows].astype(jnp.float32)
    shown = grads_ref[2 * rows :].astype(jnp.float32)
    loss_ref[...] = shown[:records] + shown[records : 2 * records]
    grad_bias_ref[...] = jnp.sum(shown[2 * records :], axis=0, keepdims=True)
    out_ref[...] = weight_ref[...].astype(jnp.float32)


def swap(parts, axis):
    return lax.all_to_all(parts, axis, 0, 0, tiled=True)


def struct(shape, dtype):
    return jax.ShapeDtypeStruct(shape, dtype)


def on_device(
    hidden_states, key_weight, queries, output_weight, code_bias, record_ids, code_labels
):
    f32, bf16 = jnp.float32, jnp.bfloat16
    records, width = code_labels.shape
    seq, label = lax.axis_size("seq"), lax.axis_size("label")
    tokens, feats = hidden_states.shape
    dims = key_weight.shape[1]
    rows = queries.shape[0]
    own_toks, own_feats = tokens // label, feats // seq

    few = pltpu.CompilerParams(vmem_limit_bytes=8 * 1024 * 1024)
    many = pltpu.CompilerParams(vmem_limit_bytes=52 * 1024 * 1024)

    vectors = lax.all_gather(jnp.stack([queries, output_weight]), "seq", axis=0)
    partial_pre = jnp.dot(hidden_states, key_weight, preferred_element_type=f32)
    pre_parts = swap(partial_pre.reshape(label, own_toks, dims), "label")
    keys_own = jnp.tanh(jnp.sum(pre_parts, axis=0)).astype(bf16)
    keys_copies = jnp.broadcast_to(keys_own[None], (label, own_toks, dims))
    keys_all = swap(keys_copies, "label").reshape(tokens, dims)

    ids = record_ids[:, None]
    leader = (lax.axis_index("seq") == 0).astype(f32).reshape(1, 1)
    held = pl.BlockSpec(memory_space=pltpu.VMEM)
    far = pl.BlockSpec(memory_space=pltpu.HBM)
    blocks = width // SPAN
    vector_scratch = pltpu.VMEM((seq, 2, rows, width), bf16)
    own_totals, totals = pl.pallas_call(
        lambda *refs: totals_kernel(records, *refs),
        in_specs=[held, far, held],
        out_specs=[held, held],
        out_shape=[
            struct((2 * records, width), f32),
            struct((seq, 4, width + LANES), f32),
        ],
        scratch_shapes=[vector_scratch, pltpu.SemaphoreType.DMA((blocks,))],
        compiler_params=many,
    )(keys_all, vectors, ids)
    totals = swap(totals, "seq")

    grads, key_grad = pl.pallas_call(
        lambda *refs: grads_kernel(records, *refs),
        in_specs=[held, far, *[held] * 6],
        out_specs=[far, held],
        out_shape=[
            struct((seq, 2 * rows + 4 * records, width), bf16),
            struct((tokens, dims), bf16),
        ],
        scratch_shapes=[
            vector_scratch,
            pltpu.VMEM((seq, 2 * rows + 4 * records, width), bf16),
            pltpu.SemaphoreType.DMA((blocks,)),
            pltpu.SemaphoreType.DMA((blocks,)),
        ],
        compiler_params=many,
    )(
        keys_all,
        vectors,
        ids,
        own_totals,
        totals,
        leader,
        code_bias[None],
        code_labels,
    )

    grads = lax.psum_scatter(grads, "seq", scatter_dimension=0)

    key_parts = swap(key_grad.reshape(label, own_toks, dims), "label")
    pre_copies = pl.pallas_call(
        pre_grad_kernel, out_shape=struct((label, own_toks, dims), bf16), compiler_params=few
    )(key_parts, keys_own)
    pre_grad = swap(pre_copies, "label").reshape(tokens, dims)
    weight_part = lax.dot_general(
        hidden_states, pre_grad, ROWS, preferred_element_type=f32
    ).astype(bf16)
    weight_parts = swap(weight_part.reshape(seq, own_feats, dims), "seq")
    weight_copies = pl.pallas_call(
        sum_kernel, out_shape=struct((seq, own_feats, dims), bf16), compiler_params=few
    )(weight_parts)
    weights = swap(weight_copies, "seq").reshape(feats, dims)
    code_loss, grad_queries, grad_output, grad_bias, grad_key_weight = pl.pallas_call(
        final_kernel,
        out_shape=[
            struct((records, width), f32),
            struct((rows, width), f32),
            struct((rows, width), f32),
            struct((1, width), f32),
            struct((feats, dims), f32),
        ],
        in_specs=[held, held],
        out_specs=[held] * 5,
        compiler_params=many,
    )(grads, weights)
    return (code_loss, grad_queries, grad_output, grad_bias[0], grad_key_weight)


def solution(mesh):
    return jax.shard_map(
        on_device,
        mesh=mesh,
        in_specs=(
            P("seq", "label"),
            P("label", None),
            P("seq", "label"),
            P("seq", "label"),
            P("label"),
            P("seq"),
            P(None, "label"),
        ),
        out_specs=(
            P(None, "label"),
            P("seq", "label"),
            P("seq", "label"),
            P("label"),
            P("label", None),
        ),
        check_vma=False,
    )
```

```python
import jax
import jax.numpy as jnp
from jax import lax
from jax.experimental import pallas as pl
from jax.experimental.pallas import tpu as pltpu
from jax.sharding import PartitionSpec as P

FAR = -1e30
ROWS = (((0,), (0,)), ((), ()))
COLS = (((1,), (1,)), ((), ()))
SPAN = 512
LANES = 128


def fetch(vectors_ref, held_ref, sems):
    blocks = []
    for low in range(0, held_ref.shape[-1], SPAN):
        codes = slice(low, low + SPAN)
        copy = pltpu.make_async_copy(
            vectors_ref.at[:, :, :, codes], held_ref.at[:, :, :, codes], sems.at[low // SPAN]
        )
        copy.start()
        blocks.append((codes, copy))
    return blocks


def products(keys, held_ref, codes):
    query_blk = held_ref[:, 0, :, codes].reshape(-1, SPAN)
    output_blk = held_ref[:, 1, :, codes].reshape(-1, SPAN)
    score_vals = jnp.dot(keys, query_blk, preferred_element_type=jnp.float32)
    value_vals = jnp.dot(keys, output_blk, preferred_element_type=jnp.float32)
    return score_vals, value_vals, query_blk, output_blk


def spread(masks, rows):
    spread_vals = rows[-1]
    for mask, row in zip(masks[:-1], rows[:-1]):
        spread_vals = jnp.where(mask, row, spread_vals)
    return spread_vals


def totals_kernel(
    records, keys_ref, vectors_ref, ids_ref, own_ref, out_ref, held_ref, sems
):
    blocks = fetch(vectors_ref, held_ref, sems)
    keys = keys_ref[...]
    ids = ids_ref[...]
    first, last = ids[:1], ids[-1:]
    single = first == last
    between = jnp.max(last - first) > 1
    heads, tails = ids == first, ids == last
    width = own_ref.shape[1]

    def totals(top, expo, weighted):
        denom = jnp.sum(expo, axis=0, keepdims=True)
        numer = jnp.sum(weighted, axis=0, keepdims=True)
        some = denom > 0.0
        safe = jnp.where(some, denom, 1.0)
        return jnp.where(some, top + jnp.log(safe), FAR), jnp.where(some, numer / safe, 0.0)

    for codes, copy in blocks:
        copy.wait()
        score_vals, value_vals, _, _ = products(keys, held_ref, codes)
        head_top = jnp.max(jnp.where(heads, score_vals, FAR), axis=0, keepdims=True)
        tail_top = jnp.max(jnp.where(tails, score_vals, FAR), axis=0, keepdims=True)
        shifted = jnp.where(heads, score_vals - head_top, score_vals - tail_top)
        expo = jnp.exp(jnp.where(jnp.logical_or(heads, tails), shifted, FAR))
        weighted = expo * value_vals
        head_expo = jnp.where(heads, expo, 0.0)
        head_weighted = jnp.where(heads, weighted, 0.0)
        head_log, head_mean = totals(head_top, head_expo, head_weighted)
        tail_log, tail_mean = totals(tail_top, expo - head_expo, weighted - head_weighted)
        table = jnp.concatenate(
            [
                head_log,
                jnp.where(single, FAR, tail_log),
                head_mean,
                jnp.where(single, 0.0, tail_mean),
            ],
            axis=0,
        )
        out_ref[:, :, codes] = jnp.broadcast_to(table[None], (out_ref.shape[0], *table.shape))

        @pl.when(between)
        def _():
            for rec in range(records):
                mask = ids == rec
                top = jnp.max(jnp.where(mask, score_vals, FAR), axis=0, keepdims=True)
                inner = jnp.where(mask, jnp.exp(jnp.where(mask, score_vals - top, FAR)), 0.0)
                log, mean = totals(top, inner, inner * value_vals)
                own_ref[rec : rec + 1, codes] = log
                own_ref[records + rec : records + rec + 1, codes] = mean

    marks = jnp.concatenate([first, last, first, last], axis=0).astype(jnp.float32)
    out_ref[:, :, width:] = jnp.broadcast_to(marks[None], (*out_ref.shape[:2], LANES))


def halves(vals):
    high = vals.astype(jnp.bfloat16).astype(jnp.float32)
    return high, vals - high


def grads_kernel(
    records,
    keys_ref,
    held_ref,
    ids_ref,
    own_ref,
    totals_ref,
    leader_ref,
    bias_ref,
    labels_ref,
    grads_ref,
    key_grad_ref,
    ready_ref,
    out_sems,
):
    keys = keys_ref[...]
    turned = keys.T
    ids = ids_ref[...]
    first, last = ids[:1], ids[-1:]
    masks = [ids == rec for rec in range(records)]
    width = own_ref.shape[1]
    parts = ready_ref.shape[0]
    rows = keys.shape[1] // parts
    widen = lambda lanes: jnp.concatenate([lanes] * (width // LANES), axis=1)
    first_marks = widen(totals_ref[:, 0, width:])
    last_marks = widen(totals_ref[:, 1, width:])
    first_logs, last_logs = totals_ref[:, 0, :width], totals_ref[:, 1, :width]
    first_means, last_means = totals_ref[:, 2, :width], totals_ref[:, 3, :width]
    logs, pools, shows = [], [], []
    for rec in range(records):
        head_logs = jnp.where(first_marks == rec, first_logs, FAR)
        tail_logs = jnp.where(last_marks == rec, last_logs, FAR)
        top = jnp.max(jnp.maximum(head_logs, tail_logs), axis=0, keepdims=True)
        head_weights, tail_weights = jnp.exp(head_logs - top), jnp.exp(tail_logs - top)
        denom = jnp.sum(head_weights + tail_weights, axis=0, keepdims=True)
        numer = jnp.sum(
            head_weights * first_means + tail_weights * last_means, axis=0, keepdims=True
        )
        inner = jnp.logical_and(first < rec, last > rec)
        own_log = own_ref[rec : rec + 1]
        own_mean = own_ref[records + rec : records + rec + 1]
        logs.append(jnp.where(inner, own_log, top + jnp.log(denom)))
        pools.append(jnp.where(inner, own_mean, numer / denom))
        shows.append(jnp.where(inner, 1.0, jnp.where(top > 0.5 * FAR, leader_ref[...], 0.0)))
    logits = jnp.concatenate(pools, axis=0) + bias_ref[...]
    labels_f = labels_ref[...].astype(jnp.float32)
    small = jnp.exp(-jnp.abs(logits))
    loss = jnp.maximum(logits, 0.0) + jnp.log1p(small) - labels_f * logits
    delta = jnp.where(logits >= 0.0, 1.0, small) / (1.0 + small) - labels_f
    show = jnp.concatenate(shows, axis=0) > 0.5
    shown = [*halves(jnp.where(show, loss, 0.0)), *halves(jnp.where(show, delta, 0.0))]
    shown = jnp.concatenate(shown, axis=0).astype(ready_ref.dtype)
    ready_ref[:, 2 * rows :, :] = jnp.broadcast_to(shown[None], (parts, *shown.shape))
    deltas = [delta[rec : rec + 1] for rec in range(records)]
    key_grad = jnp.zeros(keys.shape, jnp.float32)
    sent = []
    for low in range(0, width, SPAN):
        codes = slice(low, low + SPAN)
        score_vals, value_vals, query_blk, output_blk = products(keys, held_ref, codes)
        cut = lambda row_list: [row[:, codes] for row in row_list]
        pool_weight = spread(masks, cut(deltas)) * jnp.exp(score_vals - spread(masks, cut(logs)))
        pool_grad = pool_weight.astype(jnp.bfloat16)
        score_grad = (pool_weight * (value_vals - spread(masks, cut(pools)))).astype(jnp.bfloat16)
        for half, grad in enumerate((score_grad, pool_grad)):
            sums = jnp.dot(turned, grad, preferred_element_type=jnp.float32)
            ready_ref[:, half * rows : (half + 1) * rows, codes] = sums.astype(
                ready_ref.dtype
            ).reshape(parts, rows, SPAN)
        sent.append(
            pltpu.make_async_copy(
                ready_ref.at[:, :, codes], grads_ref.at[:, :, codes], out_sems.at[len(sent)]
            )
        )
        sent[-1].start()
        key_grad += lax.dot_general(
            score_grad, query_blk, COLS, preferred_element_type=jnp.float32
        )
        key_grad += lax.dot_general(
            pool_grad, output_blk, COLS, preferred_element_type=jnp.float32
        )
    key_grad_ref[...] = key_grad.astype(key_grad_ref.dtype)
    for copy in sent:
        copy.wait()


def pre_grad_kernel(parts_ref, keys_ref, out_ref):
    keys_f = keys_ref[...].astype(jnp.float32)
    total = jnp.sum(parts_ref[...].astype(jnp.float32), axis=0)
    own = (total * (1.0 - keys_f * keys_f)).astype(out_ref.dtype)
    out_ref[...] = jnp.broadcast_to(own[None], out_ref.shape)


def sum_kernel(parts_ref, out_ref):
    own = jnp.sum(parts_ref[...].astype(jnp.float32), axis=0).astype(out_ref.dtype)
    out_ref[...] = jnp.broadcast_to(own[None], out_ref.shape)


def final_kernel(
    grads_ref, weight_ref, loss_ref, grad_query_ref, grad_output_ref, grad_bias_ref, out_ref
):
    rows, records = grad_query_ref.shape[0], loss_ref.shape[0]
    grad_query_ref[...] = grads_ref[:rows].astype(jnp.float32)
    grad_output_ref[...] = grads_ref[rows : 2 * rows].astype(jnp.float32)
    shown = grads_ref[2 * rows :].astype(jnp.float32)
    loss_ref[...] = shown[:records] + shown[records : 2 * records]
    grad_bias_ref[...] = jnp.sum(shown[2 * records :], axis=0, keepdims=True)
    out_ref[...] = weight_ref[...].astype(jnp.float32)


def swap(parts, axis):
    return lax.all_to_all(parts, axis, 0, 0, tiled=True)


def struct(shape, dtype):
    return jax.ShapeDtypeStruct(shape, dtype)


def on_device(
    hidden_states, key_weight, queries, output_weight, code_bias, record_ids, code_labels
):
    f32, bf16 = jnp.float32, jnp.bfloat16
    records, width = code_labels.shape
    seq, label = lax.axis_size("seq"), lax.axis_size("label")
    tokens, feats = hidden_states.shape
    dims = key_weight.shape[1]
    rows = queries.shape[0]
    own_toks, own_feats = tokens // label, feats // seq

    few = pltpu.CompilerParams(vmem_limit_bytes=8 * 1024 * 1024)
    some = pltpu.CompilerParams(vmem_limit_bytes=50 * 1024 * 1024)
    many = pltpu.CompilerParams(vmem_limit_bytes=50 * 1024 * 1024)

    vectors = lax.all_gather(jnp.stack([queries, output_weight]), "seq", axis=0)
    partial_pre = jnp.dot(hidden_states, key_weight, preferred_element_type=f32)
    pre_parts = swap(partial_pre.reshape(label, own_toks, dims), "label")
    keys_own = jnp.tanh(jnp.sum(pre_parts, axis=0)).astype(bf16)
    keys_copies = jnp.broadcast_to(keys_own[None], (label, own_toks, dims))
    keys_all = swap(keys_copies, "label").reshape(tokens, dims)

    ids = record_ids[:, None]
    leader = (lax.axis_index("seq") == 0).astype(f32).reshape(1, 1)
    held = pl.BlockSpec(memory_space=pltpu.VMEM)
    far = pl.BlockSpec(memory_space=pltpu.HBM)
    blocks = width // SPAN
    own_totals, totals, vectors = pl.pallas_call(
        lambda *refs: totals_kernel(records, *refs),
        in_specs=[held, far, held],
        out_specs=[held, held, held],
        out_shape=[
            struct((2 * records, width), f32),
            struct((seq, 4, width + LANES), f32),
            struct(vectors.shape, bf16),
        ],
        scratch_shapes=[pltpu.SemaphoreType.DMA((blocks,))],
        compiler_params=many,
    )(keys_all, vectors, ids)
    totals = swap(totals, "seq")

    grads, key_grad = pl.pallas_call(
        lambda *refs: grads_kernel(records, *refs),
        in_specs=[held] * 8,
        out_specs=[far, held],
        out_shape=[
            struct((seq, 2 * rows + 4 * records, width), bf16),
            struct((tokens, dims), bf16),
        ],
        scratch_shapes=[
            pltpu.VMEM((seq, 2 * rows + 4 * records, width), bf16),
            pltpu.SemaphoreType.DMA((blocks,)),
        ],
        compiler_params=some,
    )(
        keys_all,
        vectors,
        ids,
        own_totals,
        totals,
        leader,
        code_bias[None],
        code_labels,
    )

    grads = lax.psum_scatter(grads, "seq", scatter_dimension=0)

    key_parts = swap(key_grad.reshape(label, own_toks, dims), "label")
    pre_copies = pl.pallas_call(
        pre_grad_kernel, out_shape=struct((label, own_toks, dims), bf16), compiler_params=few
    )(key_parts, keys_own)
    pre_grad = swap(pre_copies, "label").reshape(tokens, dims)
    weight_part = lax.dot_general(
        hidden_states, pre_grad, ROWS, preferred_element_type=f32
    ).astype(bf16)
    weight_parts = swap(weight_part.reshape(seq, own_feats, dims), "seq")
    weight_copies = pl.pallas_call(
        sum_kernel, out_shape=struct((seq, own_feats, dims), bf16), compiler_params=few
    )(weight_parts)
    weights = swap(weight_copies, "seq").reshape(feats, dims)
    code_loss, grad_queries, grad_output, grad_bias, grad_key_weight = pl.pallas_call(
        final_kernel,
        out_shape=[
            struct((records, width), f32),
            struct((rows, width), f32),
            struct((rows, width), f32),
            struct((1, width), f32),
            struct((feats, dims), f32),
        ],
        in_specs=[held, held],
        out_specs=[held] * 5,
        compiler_params=many,
    )(grads, weights)
    return (code_loss, grad_queries, grad_output, grad_bias[0], grad_key_weight)


def solution(mesh):
    return jax.shard_map(
        on_device,
        mesh=mesh,
        in_specs=(
            P("seq", "label"),
            P("label", None),
            P("seq", "label"),
            P("seq", "label"),
            P("label"),
            P("seq"),
            P(None, "label"),
        ),
        out_specs=(
            P(None, "label"),
            P("seq", "label"),
            P("seq", "label"),
            P("label"),
            P("label", None),
        ),
        check_vma=False,
    )
```

```python
import jax
import jax.numpy as jnp
from jax import lax
from jax.experimental import pallas as pl
from jax.experimental.pallas import tpu as pltpu
from jax.sharding import PartitionSpec as P

FAR = -1e30
ROWS = (((0,), (0,)), ((), ()))
COLS = (((1,), (1,)), ((), ()))
SPAN = 512
LANES = 128


def fetch(vectors_ref, held_ref, sems):
    blocks = []
    for low in range(0, held_ref.shape[-1], SPAN):
        codes = slice(low, low + SPAN)
        copy = pltpu.make_async_copy(
            vectors_ref.at[:, :, :, codes], held_ref.at[:, :, :, codes], sems.at[low // SPAN]
        )
        copy.start()
        blocks.append((codes, copy))
    return blocks


def products(keys, held_ref, codes):
    query_blk = held_ref[:, 0, :, codes].reshape(-1, SPAN)
    output_blk = held_ref[:, 1, :, codes].reshape(-1, SPAN)
    score_vals = jnp.dot(keys, query_blk, preferred_element_type=jnp.float32)
    value_vals = jnp.dot(keys, output_blk, preferred_element_type=jnp.float32)
    return score_vals, value_vals, query_blk, output_blk


def spread(masks, rows):
    spread_vals = rows[-1]
    for mask, row in zip(masks[:-1], rows[:-1]):
        spread_vals = jnp.where(mask, row, spread_vals)
    return spread_vals


def totals_kernel(
    records, keys_ref, vectors_ref, ids_ref, own_ref, out_ref, held_ref, sems
):
    blocks = fetch(vectors_ref, held_ref, sems)
    keys = keys_ref[...]
    ids = ids_ref[...]
    first, last = ids[:1], ids[-1:]
    single = first == last
    between = jnp.max(last - first) > 1
    heads, tails = ids == first, ids == last
    width = own_ref.shape[1]

    def totals(top, expo, weighted):
        denom = jnp.sum(expo, axis=0, keepdims=True)
        numer = jnp.sum(weighted, axis=0, keepdims=True)
        some = denom > 0.0
        safe = jnp.where(some, denom, 1.0)
        return jnp.where(some, top + jnp.log(safe), FAR), jnp.where(some, numer / safe, 0.0)

    for codes, copy in blocks:
        copy.wait()
        score_vals, value_vals, _, _ = products(keys, held_ref, codes)
        head_top = jnp.max(jnp.where(heads, score_vals, FAR), axis=0, keepdims=True)
        tail_top = jnp.max(jnp.where(tails, score_vals, FAR), axis=0, keepdims=True)
        shifted = jnp.where(heads, score_vals - head_top, score_vals - tail_top)
        expo = jnp.exp(jnp.where(jnp.logical_or(heads, tails), shifted, FAR))
        weighted = expo * value_vals
        head_expo = jnp.where(heads, expo, 0.0)
        head_weighted = jnp.where(heads, weighted, 0.0)
        head_log, head_mean = totals(head_top, head_expo, head_weighted)
        tail_log, tail_mean = totals(tail_top, expo - head_expo, weighted - head_weighted)
        table = jnp.concatenate(
            [
                head_log,
                jnp.where(single, FAR, tail_log),
                head_mean,
                jnp.where(single, 0.0, tail_mean),
            ],
            axis=0,
        )
        out_ref[:, :, codes] = jnp.broadcast_to(table[None], (out_ref.shape[0], *table.shape))

        @pl.when(between)
        def _():
            for rec in range(records):
                mask = ids == rec
                top = jnp.max(jnp.where(mask, score_vals, FAR), axis=0, keepdims=True)
                inner = jnp.where(mask, jnp.exp(jnp.where(mask, score_vals - top, FAR)), 0.0)
                log, mean = totals(top, inner, inner * value_vals)
                own_ref[rec : rec + 1, codes] = log
                own_ref[records + rec : records + rec + 1, codes] = mean

    marks = jnp.concatenate([first, last, first, last], axis=0).astype(jnp.float32)
    out_ref[:, :, width:] = jnp.broadcast_to(marks[None], (*out_ref.shape[:2], LANES))


def halves(vals):
    high = vals.astype(jnp.bfloat16).astype(jnp.float32)
    return high, vals - high


def grads_kernel(
    records,
    keys_ref,
    held_ref,
    ids_ref,
    own_ref,
    totals_ref,
    leader_ref,
    bias_ref,
    labels_ref,
    grads_ref,
    key_grad_ref,
    ready_ref,
    out_sems,
):
    keys = keys_ref[...]
    turned = keys.T
    ids = ids_ref[...]
    first, last = ids[:1], ids[-1:]
    masks = [ids == rec for rec in range(records)]
    width = own_ref.shape[1]
    parts = ready_ref.shape[0]
    rows = keys.shape[1] // parts
    widen = lambda lanes: jnp.concatenate([lanes] * (width // LANES), axis=1)
    first_marks = widen(totals_ref[:, 0, width:])
    last_marks = widen(totals_ref[:, 1, width:])
    first_logs, last_logs = totals_ref[:, 0, :width], totals_ref[:, 1, :width]
    first_means, last_means = totals_ref[:, 2, :width], totals_ref[:, 3, :width]
    logs, pools, shows = [], [], []
    for rec in range(records):
        head_logs = jnp.where(first_marks == rec, first_logs, FAR)
        tail_logs = jnp.where(last_marks == rec, last_logs, FAR)
        top = jnp.max(jnp.maximum(head_logs, tail_logs), axis=0, keepdims=True)
        head_weights, tail_weights = jnp.exp(head_logs - top), jnp.exp(tail_logs - top)
        denom = jnp.sum(head_weights + tail_weights, axis=0, keepdims=True)
        numer = jnp.sum(
            head_weights * first_means + tail_weights * last_means, axis=0, keepdims=True
        )
        inner = jnp.logical_and(first < rec, last > rec)
        own_log = own_ref[rec : rec + 1]
        own_mean = own_ref[records + rec : records + rec + 1]
        logs.append(jnp.where(inner, own_log, top + jnp.log(denom)))
        pools.append(jnp.where(inner, own_mean, numer / denom))
        shows.append(jnp.where(inner, 1.0, jnp.where(top > 0.5 * FAR, leader_ref[...], 0.0)))
    logits = jnp.concatenate(pools, axis=0) + bias_ref[...]
    labels_f = labels_ref[...].astype(jnp.float32)
    small = jnp.exp(-jnp.abs(logits))
    loss = jnp.maximum(logits, 0.0) + jnp.log1p(small) - labels_f * logits
    delta = jnp.where(logits >= 0.0, 1.0, small) / (1.0 + small) - labels_f
    show = jnp.concatenate(shows, axis=0) > 0.5
    shown = [*halves(jnp.where(show, loss, 0.0)), *halves(jnp.where(show, delta, 0.0))]
    shown = jnp.concatenate(shown, axis=0).astype(ready_ref.dtype)
    ready_ref[:, 2 * rows :, :] = jnp.broadcast_to(shown[None], (parts, *shown.shape))
    deltas = [delta[rec : rec + 1] for rec in range(records)]
    def apply(over):
        key_grad = jnp.zeros(keys.shape, jnp.float32)
        sent = []
        for low in range(0, width, SPAN):
            codes = slice(low, low + SPAN)
            score_vals, value_vals, query_blk, output_blk = products(keys, held_ref, codes)
            cut = lambda row_list: [row[:, codes] for row in row_list]
            pool_weight = over(cut(deltas)) * jnp.exp(score_vals - over(cut(logs)))
            pool_grad = pool_weight.astype(jnp.bfloat16)
            score_grad = (pool_weight * (value_vals - over(cut(pools)))).astype(jnp.bfloat16)
            for half, grad in enumerate((score_grad, pool_grad)):
                sums = jnp.dot(turned, grad, preferred_element_type=jnp.float32)
                ready_ref[:, half * rows : (half + 1) * rows, codes] = sums.astype(
                    ready_ref.dtype
                ).reshape(parts, rows, SPAN)
            sent.append(
                pltpu.make_async_copy(
                    ready_ref.at[:, :, codes], grads_ref.at[:, :, codes], out_sems.at[len(sent)]
                )
            )
            sent[-1].start()
            key_grad += lax.dot_general(
                score_grad, query_blk, COLS, preferred_element_type=jnp.float32
            )
            key_grad += lax.dot_general(
                pool_grad, output_blk, COLS, preferred_element_type=jnp.float32
            )
        key_grad_ref[...] = key_grad.astype(key_grad_ref.dtype)
        for copy in sent:
            copy.wait()

    between = jnp.max(last - first) > 1
    heads = ids == first

    def ends(row_list):
        picked = []
        for end in (first, last):
            row = row_list[-1]
            for rec in range(records - 1):
                row = jnp.where(end == rec, row_list[rec], row)
            picked.append(row)
        return jnp.where(heads, *picked)

    pl.when(between)(lambda: apply(lambda row_list: spread(masks, row_list)))
    pl.when(jnp.logical_not(between))(lambda: apply(ends))


def pre_grad_kernel(parts_ref, keys_ref, out_ref):
    keys_f = keys_ref[...].astype(jnp.float32)
    total = jnp.sum(parts_ref[...].astype(jnp.float32), axis=0)
    own = (total * (1.0 - keys_f * keys_f)).astype(out_ref.dtype)
    out_ref[...] = jnp.broadcast_to(own[None], out_ref.shape)


def sum_kernel(parts_ref, out_ref):
    own = jnp.sum(parts_ref[...].astype(jnp.float32), axis=0).astype(out_ref.dtype)
    out_ref[...] = jnp.broadcast_to(own[None], out_ref.shape)


def final_kernel(
    grads_ref, weight_ref, loss_ref, grad_query_ref, grad_output_ref, grad_bias_ref, out_ref
):
    rows, records = grad_query_ref.shape[0], loss_ref.shape[0]
    grad_query_ref[...] = grads_ref[:rows].astype(jnp.float32)
    grad_output_ref[...] = grads_ref[rows : 2 * rows].astype(jnp.float32)
    shown = grads_ref[2 * rows :].astype(jnp.float32)
    loss_ref[...] = shown[:records] + shown[records : 2 * records]
    grad_bias_ref[...] = jnp.sum(shown[2 * records :], axis=0, keepdims=True)
    out_ref[...] = weight_ref[...].astype(jnp.float32)


def swap(parts, axis):
    return lax.all_to_all(parts, axis, 0, 0, tiled=True)


def struct(shape, dtype):
    return jax.ShapeDtypeStruct(shape, dtype)


def on_device(
    hidden_states, key_weight, queries, output_weight, code_bias, record_ids, code_labels
):
    f32, bf16 = jnp.float32, jnp.bfloat16
    records, width = code_labels.shape
    seq, label = lax.axis_size("seq"), lax.axis_size("label")
    tokens, feats = hidden_states.shape
    dims = key_weight.shape[1]
    rows = queries.shape[0]
    own_toks, own_feats = tokens // label, feats // seq

    few = pltpu.CompilerParams(vmem_limit_bytes=8 * 1024 * 1024)
    some = pltpu.CompilerParams(vmem_limit_bytes=50 * 1024 * 1024)
    many = pltpu.CompilerParams(vmem_limit_bytes=50 * 1024 * 1024)

    vectors = lax.all_gather(jnp.stack([queries, output_weight]), "seq", axis=0)
    partial_pre = jnp.dot(hidden_states, key_weight, preferred_element_type=f32)
    pre_parts = swap(partial_pre.reshape(label, own_toks, dims), "label")
    keys_own = jnp.tanh(jnp.sum(pre_parts, axis=0)).astype(bf16)
    keys_copies = jnp.broadcast_to(keys_own[None], (label, own_toks, dims))
    keys_all = swap(keys_copies, "label").reshape(tokens, dims)

    ids = record_ids[:, None]
    leader = (lax.axis_index("seq") == 0).astype(f32).reshape(1, 1)
    held = pl.BlockSpec(memory_space=pltpu.VMEM)
    far = pl.BlockSpec(memory_space=pltpu.HBM)
    blocks = width // SPAN
    own_totals, totals, vectors = pl.pallas_call(
        lambda *refs: totals_kernel(records, *refs),
        in_specs=[held, far, held],
        out_specs=[held, held, held],
        out_shape=[
            struct((2 * records, width), f32),
            struct((seq, 4, width + LANES), f32),
            struct(vectors.shape, bf16),
        ],
        scratch_shapes=[pltpu.SemaphoreType.DMA((blocks,))],
        compiler_params=many,
    )(keys_all, vectors, ids)
    totals = swap(totals, "seq")

    grads, key_grad = pl.pallas_call(
        lambda *refs: grads_kernel(records, *refs),
        in_specs=[held] * 8,
        out_specs=[far, held],
        out_shape=[
            struct((seq, 2 * rows + 4 * records, width), bf16),
            struct((tokens, dims), bf16),
        ],
        scratch_shapes=[
            pltpu.VMEM((seq, 2 * rows + 4 * records, width), bf16),
            pltpu.SemaphoreType.DMA((blocks,)),
        ],
        compiler_params=some,
    )(
        keys_all,
        vectors,
        ids,
        own_totals,
        totals,
        leader,
        code_bias[None],
        code_labels,
    )

    grads = lax.psum_scatter(grads, "seq", scatter_dimension=0)

    key_parts = swap(key_grad.reshape(label, own_toks, dims), "label")
    pre_copies = pl.pallas_call(
        pre_grad_kernel, out_shape=struct((label, own_toks, dims), bf16), compiler_params=few
    )(key_parts, keys_own)
    pre_grad = swap(pre_copies, "label").reshape(tokens, dims)
    weight_part = lax.dot_general(
        hidden_states, pre_grad, ROWS, preferred_element_type=f32
    ).astype(bf16)
    weight_parts = swap(weight_part.reshape(seq, own_feats, dims), "seq")
    weight_copies = pl.pallas_call(
        sum_kernel, out_shape=struct((seq, own_feats, dims), bf16), compiler_params=few
    )(weight_parts)
    weights = swap(weight_copies, "seq").reshape(feats, dims)
    code_loss, grad_queries, grad_output, grad_bias, grad_key_weight = pl.pallas_call(
        final_kernel,
        out_shape=[
            struct((records, width), f32),
            struct((rows, width), f32),
            struct((rows, width), f32),
            struct((1, width), f32),
            struct((feats, dims), f32),
        ],
        in_specs=[held, held],
        out_specs=[held] * 5,
        compiler_params=many,
    )(grads, weights)
    return (code_loss, grad_queries, grad_output, grad_bias[0], grad_key_weight)


def solution(mesh):
    return jax.shard_map(
        on_device,
        mesh=mesh,
        in_specs=(
            P("seq", "label"),
            P("label", None),
            P("seq", "label"),
            P("seq", "label"),
            P("label"),
            P("seq"),
            P(None, "label"),
        ),
        out_specs=(
            P(None, "label"),
            P("seq", "label"),
            P("seq", "label"),
            P("label"),
            P("label", None),
        ),
        check_vma=False,
    )
```

```python
import jax
import jax.numpy as jnp
from jax import lax
from jax.experimental import pallas as pl
from jax.experimental.pallas import tpu as pltpu
from jax.sharding import PartitionSpec as P

FAR = -1e30
ROWS = (((0,), (0,)), ((), ()))
COLS = (((1,), (1,)), ((), ()))
SPAN = 512
LANES = 128


def fetch(vectors_ref, held_ref, sems):
    blocks = []
    for low in range(0, held_ref.shape[-1], SPAN):
        codes = slice(low, low + SPAN)
        copy = pltpu.make_async_copy(
            vectors_ref.at[:, :, :, codes], held_ref.at[:, :, :, codes], sems.at[low // SPAN]
        )
        copy.start()
        blocks.append((codes, copy))
    return blocks


def products(keys, held_ref, codes):
    query_blk = held_ref[:, 0, :, codes].reshape(-1, SPAN)
    output_blk = held_ref[:, 1, :, codes].reshape(-1, SPAN)
    score_vals = jnp.dot(keys, query_blk, preferred_element_type=jnp.float32)
    value_vals = jnp.dot(keys, output_blk, preferred_element_type=jnp.float32)
    return score_vals, value_vals, query_blk, output_blk


def spread(masks, rows):
    spread_vals = rows[-1]
    for mask, row in zip(masks[:-1], rows[:-1]):
        spread_vals = jnp.where(mask, row, spread_vals)
    return spread_vals


def totals_kernel(
    records, keys_ref, vectors_ref, ids_ref, own_ref, out_ref, held_ref, sems
):
    blocks = fetch(vectors_ref, held_ref, sems)
    keys = keys_ref[...]
    ids = ids_ref[...]
    first, last = ids[:1], ids[-1:]
    single = first == last
    between = jnp.max(last - first) > 1
    heads, tails = ids == first, ids == last
    width = own_ref.shape[1]

    def totals(top, expo, weighted):
        denom = jnp.sum(expo, axis=0, keepdims=True)
        numer = jnp.sum(weighted, axis=0, keepdims=True)
        some = denom > 0.0
        safe = jnp.where(some, denom, 1.0)
        return jnp.where(some, top + jnp.log(safe), FAR), jnp.where(some, numer / safe, 0.0)

    for codes, copy in blocks:
        copy.wait()
        score_vals, value_vals, _, _ = products(keys, held_ref, codes)
        head_top = jnp.max(jnp.where(heads, score_vals, FAR), axis=0, keepdims=True)
        tail_top = jnp.max(jnp.where(tails, score_vals, FAR), axis=0, keepdims=True)
        shifted = jnp.where(heads, score_vals - head_top, score_vals - tail_top)
        expo = jnp.exp(jnp.where(jnp.logical_or(heads, tails), shifted, FAR))
        weighted = expo * value_vals
        head_expo = jnp.where(heads, expo, 0.0)
        head_weighted = jnp.where(heads, weighted, 0.0)
        head_log, head_mean = totals(head_top, head_expo, head_weighted)
        tail_log, tail_mean = totals(tail_top, expo - head_expo, weighted - head_weighted)
        table = jnp.concatenate(
            [
                head_log,
                jnp.where(single, FAR, tail_log),
                head_mean,
                jnp.where(single, 0.0, tail_mean),
            ],
            axis=0,
        )
        out_ref[:, :, codes] = jnp.broadcast_to(table[None], (out_ref.shape[0], *table.shape))

        @pl.when(between)
        def _():
            for rec in range(records):
                mask = ids == rec
                top = jnp.max(jnp.where(mask, score_vals, FAR), axis=0, keepdims=True)
                inner = jnp.where(mask, jnp.exp(jnp.where(mask, score_vals - top, FAR)), 0.0)
                log, mean = totals(top, inner, inner * value_vals)
                own_ref[rec : rec + 1, codes] = log
                own_ref[records + rec : records + rec + 1, codes] = mean

    marks = jnp.concatenate([first, last, first, last], axis=0).astype(jnp.float32)
    out_ref[:, :, width:] = jnp.broadcast_to(marks[None], (*out_ref.shape[:2], LANES))


def halves(vals):
    high = vals.astype(jnp.bfloat16).astype(jnp.float32)
    return high, vals - high


def grads_kernel(
    records,
    keys_ref,
    held_ref,
    ids_ref,
    own_ref,
    totals_ref,
    leader_ref,
    bias_ref,
    labels_ref,
    grads_ref,
    key_grad_ref,
    ready_ref,
    out_sems,
):
    keys = keys_ref[...]
    turned = keys.T
    ids = ids_ref[...]
    first, last = ids[:1], ids[-1:]
    masks = [ids == rec for rec in range(records)]
    width = own_ref.shape[1]
    parts = ready_ref.shape[0]
    rows = keys.shape[1] // parts
    widen = lambda lanes: jnp.concatenate([lanes] * (width // LANES), axis=1)
    first_marks = widen(totals_ref[:, 0, width:])
    last_marks = widen(totals_ref[:, 1, width:])
    first_logs, last_logs = totals_ref[:, 0, :width], totals_ref[:, 1, :width]
    first_means, last_means = totals_ref[:, 2, :width], totals_ref[:, 3, :width]
    logs, pools, shows = [], [], []
    for rec in range(records):
        head_logs = jnp.where(first_marks == rec, first_logs, FAR)
        tail_logs = jnp.where(last_marks == rec, last_logs, FAR)
        top = jnp.max(jnp.maximum(head_logs, tail_logs), axis=0, keepdims=True)
        head_weights, tail_weights = jnp.exp(head_logs - top), jnp.exp(tail_logs - top)
        denom = jnp.sum(head_weights + tail_weights, axis=0, keepdims=True)
        numer = jnp.sum(
            head_weights * first_means + tail_weights * last_means, axis=0, keepdims=True
        )
        inner = jnp.logical_and(first < rec, last > rec)
        own_log = own_ref[rec : rec + 1]
        own_mean = own_ref[records + rec : records + rec + 1]
        logs.append(jnp.where(inner, own_log, top + jnp.log(denom)))
        pools.append(jnp.where(inner, own_mean, numer / denom))
        shows.append(jnp.where(inner, 1.0, jnp.where(top > 0.5 * FAR, leader_ref[...], 0.0)))
    logits = jnp.concatenate(pools, axis=0) + bias_ref[...]
    labels_f = labels_ref[...].astype(jnp.float32)
    small = jnp.exp(-jnp.abs(logits))
    loss = jnp.maximum(logits, 0.0) + jnp.log1p(small) - labels_f * logits
    delta = jnp.where(logits >= 0.0, 1.0, small) / (1.0 + small) - labels_f
    show = jnp.concatenate(shows, axis=0) > 0.5
    shown = [*halves(jnp.where(show, loss, 0.0)), *halves(jnp.where(show, delta, 0.0))]
    shown = jnp.concatenate(shown, axis=0).astype(ready_ref.dtype)
    ready_ref[:, 2 * rows :, :] = jnp.broadcast_to(shown[None], (parts, *shown.shape))
    deltas = [delta[rec : rec + 1] for rec in range(records)]
    def apply(over):
        key_grad = jnp.zeros(keys.shape, jnp.float32)
        sent = []
        for low in range(0, width, SPAN):
            codes = slice(low, low + SPAN)
            score_vals, value_vals, query_blk, output_blk = products(keys, held_ref, codes)
            cut = lambda row_list: [row[:, codes] for row in row_list]
            pool_weight = over(cut(deltas)) * jnp.exp(score_vals - over(cut(logs)))
            pool_grad = pool_weight.astype(jnp.bfloat16)
            score_grad = (pool_weight * (value_vals - over(cut(pools)))).astype(jnp.bfloat16)
            for half, grad in enumerate((score_grad, pool_grad)):
                sums = jnp.dot(turned, grad, preferred_element_type=jnp.float32)
                ready_ref[:, half * rows : (half + 1) * rows, codes] = sums.astype(
                    ready_ref.dtype
                ).reshape(parts, rows, SPAN)
            sent.append(
                pltpu.make_async_copy(
                    ready_ref.at[:, :, codes], grads_ref.at[:, :, codes], out_sems.at[len(sent)]
                )
            )
            sent[-1].start()
            key_grad += lax.dot_general(
                jnp.concatenate([score_grad, pool_grad], axis=1),
                jnp.concatenate([query_blk, output_blk], axis=1),
                COLS,
                preferred_element_type=jnp.float32,
            )
        key_grad_ref[...] = key_grad.astype(key_grad_ref.dtype)
        for copy in sent:
            copy.wait()

    between = jnp.max(last - first) > 1
    heads = ids == first

    def ends(row_list):
        picked = []
        for end in (first, last):
            row = row_list[-1]
            for rec in range(records - 1):
                row = jnp.where(end == rec, row_list[rec], row)
            picked.append(row)
        return jnp.where(heads, *picked)

    pl.when(between)(lambda: apply(lambda row_list: spread(masks, row_list)))
    pl.when(jnp.logical_not(between))(lambda: apply(ends))


def pre_grad_kernel(parts_ref, keys_ref, out_ref):
    keys_f = keys_ref[...].astype(jnp.float32)
    total = jnp.sum(parts_ref[...].astype(jnp.float32), axis=0)
    own = (total * (1.0 - keys_f * keys_f)).astype(out_ref.dtype)
    out_ref[...] = jnp.broadcast_to(own[None], out_ref.shape)


def sum_kernel(parts_ref, out_ref):
    own = jnp.sum(parts_ref[...].astype(jnp.float32), axis=0).astype(out_ref.dtype)
    out_ref[...] = jnp.broadcast_to(own[None], out_ref.shape)


def final_kernel(
    grads_ref, weight_ref, loss_ref, grad_query_ref, grad_output_ref, grad_bias_ref, out_ref
):
    rows, records = grad_query_ref.shape[0], loss_ref.shape[0]
    grad_query_ref[...] = grads_ref[:rows].astype(jnp.float32)
    grad_output_ref[...] = grads_ref[rows : 2 * rows].astype(jnp.float32)
    shown = grads_ref[2 * rows :].astype(jnp.float32)
    loss_ref[...] = shown[:records] + shown[records : 2 * records]
    grad_bias_ref[...] = jnp.sum(shown[2 * records :], axis=0, keepdims=True)
    out_ref[...] = weight_ref[...].astype(jnp.float32)


def swap(parts, axis):
    return lax.all_to_all(parts, axis, 0, 0, tiled=True)


def struct(shape, dtype):
    return jax.ShapeDtypeStruct(shape, dtype)


def on_device(
    hidden_states, key_weight, queries, output_weight, code_bias, record_ids, code_labels
):
    f32, bf16 = jnp.float32, jnp.bfloat16
    records, width = code_labels.shape
    seq, label = lax.axis_size("seq"), lax.axis_size("label")
    tokens, feats = hidden_states.shape
    dims = key_weight.shape[1]
    rows = queries.shape[0]
    own_toks, own_feats = tokens // label, feats // seq

    few = pltpu.CompilerParams(vmem_limit_bytes=8 * 1024 * 1024)
    some = pltpu.CompilerParams(vmem_limit_bytes=50 * 1024 * 1024)
    many = pltpu.CompilerParams(vmem_limit_bytes=50 * 1024 * 1024)

    vectors = lax.all_gather(jnp.stack([queries, output_weight]), "seq", axis=0)
    partial_pre = jnp.dot(hidden_states, key_weight, preferred_element_type=f32)
    pre_parts = swap(partial_pre.reshape(label, own_toks, dims), "label")
    keys_own = jnp.tanh(jnp.sum(pre_parts, axis=0)).astype(bf16)
    keys_copies = jnp.broadcast_to(keys_own[None], (label, own_toks, dims))
    keys_all = swap(keys_copies, "label").reshape(tokens, dims)

    ids = record_ids[:, None]
    leader = (lax.axis_index("seq") == 0).astype(f32).reshape(1, 1)
    held = pl.BlockSpec(memory_space=pltpu.VMEM)
    far = pl.BlockSpec(memory_space=pltpu.HBM)
    blocks = width // SPAN
    own_totals, totals, vectors = pl.pallas_call(
        lambda *refs: totals_kernel(records, *refs),
        in_specs=[held, far, held],
        out_specs=[held, held, held],
        out_shape=[
            struct((2 * records, width), f32),
            struct((seq, 4, width + LANES), f32),
            struct(vectors.shape, bf16),
        ],
        scratch_shapes=[pltpu.SemaphoreType.DMA((blocks,))],
        compiler_params=many,
    )(keys_all, vectors, ids)
    totals = swap(totals, "seq")

    grads, key_grad = pl.pallas_call(
        lambda *refs: grads_kernel(records, *refs),
        in_specs=[held] * 8,
        out_specs=[far, held],
        out_shape=[
            struct((seq, 2 * rows + 4 * records, width), bf16),
            struct((tokens, dims), bf16),
        ],
        scratch_shapes=[
            pltpu.VMEM((seq, 2 * rows + 4 * records, width), bf16),
            pltpu.SemaphoreType.DMA((blocks,)),
        ],
        compiler_params=some,
    )(
        keys_all,
        vectors,
        ids,
        own_totals,
        totals,
        leader,
        code_bias[None],
        code_labels,
    )

    grads = lax.psum_scatter(grads, "seq", scatter_dimension=0)

    key_parts = swap(key_grad.reshape(label, own_toks, dims), "label")
    pre_copies = pl.pallas_call(
        pre_grad_kernel, out_shape=struct((label, own_toks, dims), bf16), compiler_params=few
    )(key_parts, keys_own)
    pre_grad = swap(pre_copies, "label").reshape(tokens, dims)
    weight_part = lax.dot_general(
        hidden_states, pre_grad, ROWS, preferred_element_type=f32
    ).astype(bf16)
    weight_parts = swap(weight_part.reshape(seq, own_feats, dims), "seq")
    weight_copies = pl.pallas_call(
        sum_kernel, out_shape=struct((seq, own_feats, dims), bf16), compiler_params=few
    )(weight_parts)
    weights = swap(weight_copies, "seq").reshape(feats, dims)
    code_loss, grad_queries, grad_output, grad_bias, grad_key_weight = pl.pallas_call(
        final_kernel,
        out_shape=[
            struct((records, width), f32),
            struct((rows, width), f32),
            struct((rows, width), f32),
            struct((1, width), f32),
            struct((feats, dims), f32),
        ],
        in_specs=[held, held],
        out_specs=[held] * 5,
        compiler_params=many,
    )(grads, weights)
    return (code_loss, grad_queries, grad_output, grad_bias[0], grad_key_weight)


def solution(mesh):
    return jax.shard_map(
        on_device,
        mesh=mesh,
        in_specs=(
            P("seq", "label"),
            P("label", None),
            P("seq", "label"),
            P("seq", "label"),
            P("label"),
            P("seq"),
            P(None, "label"),
        ),
        out_specs=(
            P(None, "label"),
            P("seq", "label"),
            P("seq", "label"),
            P("label"),
            P("label", None),
        ),
        check_vma=False,
    )
```

```python
import jax
import jax.numpy as jnp
from jax import lax
from jax.experimental import pallas as pl
from jax.experimental.pallas import tpu as pltpu
from jax.sharding import PartitionSpec as P

FAR = -1e30
ROWS = (((0,), (0,)), ((), ()))
COLS = (((1,), (1,)), ((), ()))
SPAN = 512
LANES = 128


def fetch(vectors_ref, held_ref, sems):
    blocks = []
    for low in range(0, held_ref.shape[-1], SPAN):
        codes = slice(low, low + SPAN)
        copy = pltpu.make_async_copy(
            vectors_ref.at[:, :, :, codes], held_ref.at[:, :, :, codes], sems.at[low // SPAN]
        )
        copy.start()
        blocks.append((codes, copy))
    return blocks


def products(keys, held_ref, codes):
    query_blk = held_ref[:, 0, :, codes].reshape(-1, SPAN)
    output_blk = held_ref[:, 1, :, codes].reshape(-1, SPAN)
    score_vals = jnp.dot(keys, query_blk, preferred_element_type=jnp.float32)
    value_vals = jnp.dot(keys, output_blk, preferred_element_type=jnp.float32)
    return score_vals, value_vals, query_blk, output_blk


def spread(masks, rows):
    spread_vals = rows[-1]
    for mask, row in zip(masks[:-1], rows[:-1]):
        spread_vals = jnp.where(mask, row, spread_vals)
    return spread_vals


def totals_kernel(
    records, keys_ref, vectors_ref, ids_ref, own_ref, out_ref, held_ref, sems
):
    blocks = fetch(vectors_ref, held_ref, sems)
    keys = keys_ref[...]
    ids = ids_ref[...]
    first, last = ids[:1], ids[-1:]
    single = first == last
    between = jnp.max(last - first) > 1
    heads, tails = ids == first, ids == last
    width = own_ref.shape[1]

    def totals(top, expo, weighted):
        denom = jnp.sum(expo, axis=0, keepdims=True)
        numer = jnp.sum(weighted, axis=0, keepdims=True)
        some = denom > 0.0
        safe = jnp.where(some, denom, 1.0)
        return jnp.where(some, top + jnp.log(safe), FAR), jnp.where(some, numer / safe, 0.0)

    for codes, copy in blocks:
        copy.wait()
        score_vals, value_vals, _, _ = products(keys, held_ref, codes)
        head_top = jnp.max(jnp.where(heads, score_vals, FAR), axis=0, keepdims=True)
        tail_top = jnp.max(jnp.where(tails, score_vals, FAR), axis=0, keepdims=True)
        shifted = jnp.where(heads, score_vals - head_top, score_vals - tail_top)
        expo = jnp.exp(jnp.where(jnp.logical_or(heads, tails), shifted, FAR))
        weighted = expo * value_vals
        head_expo = jnp.where(heads, expo, 0.0)
        head_weighted = jnp.where(heads, weighted, 0.0)
        head_log, head_mean = totals(head_top, head_expo, head_weighted)
        tail_log, tail_mean = totals(tail_top, expo - head_expo, weighted - head_weighted)
        table = jnp.concatenate(
            [
                head_log,
                jnp.where(single, FAR, tail_log),
                head_mean,
                jnp.where(single, 0.0, tail_mean),
            ],
            axis=0,
        )
        out_ref[:, :, codes] = jnp.broadcast_to(table[None], (out_ref.shape[0], *table.shape))

        @pl.when(between)
        def _():
            for rec in range(records):
                mask = ids == rec
                top = jnp.max(jnp.where(mask, score_vals, FAR), axis=0, keepdims=True)
                inner = jnp.where(mask, jnp.exp(jnp.where(mask, score_vals - top, FAR)), 0.0)
                log, mean = totals(top, inner, inner * value_vals)
                own_ref[rec : rec + 1, codes] = log
                own_ref[records + rec : records + rec + 1, codes] = mean

    marks = jnp.concatenate([first, last, first, last], axis=0).astype(jnp.float32)
    out_ref[:, :, width:] = jnp.broadcast_to(marks[None], (*out_ref.shape[:2], LANES))


def halves(vals):
    high = vals.astype(jnp.bfloat16).astype(jnp.float32)
    return high, vals - high


def grads_kernel(
    records,
    keys_ref,
    held_ref,
    ids_ref,
    own_ref,
    totals_ref,
    leader_ref,
    bias_ref,
    labels_ref,
    grads_ref,
    key_grad_ref,
    ready_ref,
    out_sems,
):
    keys = keys_ref[...]
    turned = keys.T
    ids = ids_ref[...]
    first, last = ids[:1], ids[-1:]
    masks = [ids == rec for rec in range(records)]
    width = own_ref.shape[1]
    parts = ready_ref.shape[0]
    rows = keys.shape[1] // parts
    widen = lambda lanes: jnp.concatenate([lanes] * (width // LANES), axis=1)
    first_marks = widen(totals_ref[:, 0, width:])
    last_marks = widen(totals_ref[:, 1, width:])
    first_logs, last_logs = totals_ref[:, 0, :width], totals_ref[:, 1, :width]
    first_means, last_means = totals_ref[:, 2, :width], totals_ref[:, 3, :width]
    logs, pools, shows = [], [], []
    for rec in range(records):
        head_logs = jnp.where(first_marks == rec, first_logs, FAR)
        tail_logs = jnp.where(last_marks == rec, last_logs, FAR)
        top = jnp.max(jnp.maximum(head_logs, tail_logs), axis=0, keepdims=True)
        head_weights, tail_weights = jnp.exp(head_logs - top), jnp.exp(tail_logs - top)
        denom = jnp.sum(head_weights + tail_weights, axis=0, keepdims=True)
        numer = jnp.sum(
            head_weights * first_means + tail_weights * last_means, axis=0, keepdims=True
        )
        inner = jnp.logical_and(first < rec, last > rec)
        own_log = own_ref[rec : rec + 1]
        own_mean = own_ref[records + rec : records + rec + 1]
        logs.append(jnp.where(inner, own_log, top + jnp.log(denom)))
        pools.append(jnp.where(inner, own_mean, numer / denom))
        shows.append(jnp.where(inner, 1.0, jnp.where(top > 0.5 * FAR, leader_ref[...], 0.0)))
    logits = jnp.concatenate(pools, axis=0) + bias_ref[...]
    labels_f = labels_ref[...].astype(jnp.float32)
    small = jnp.exp(-jnp.abs(logits))
    loss = jnp.maximum(logits, 0.0) + jnp.log1p(small) - labels_f * logits
    delta = jnp.where(logits >= 0.0, 1.0, small) / (1.0 + small) - labels_f
    show = jnp.concatenate(shows, axis=0) > 0.5
    shown = [*halves(jnp.where(show, loss, 0.0)), *halves(jnp.where(show, delta, 0.0))]
    shown = jnp.concatenate(shown, axis=0).astype(ready_ref.dtype)
    ready_ref[:, 2 * rows :, :] = jnp.broadcast_to(shown[None], (parts, *shown.shape))
    deltas = [delta[rec : rec + 1] for rec in range(records)]
    def apply(over):
        key_grad = jnp.zeros(keys.shape, jnp.float32)
        sent = []
        for low in range(0, width, SPAN):
            codes = slice(low, low + SPAN)
            score_vals, value_vals, query_blk, output_blk = products(keys, held_ref, codes)
            cut = lambda row_list: [row[:, codes] for row in row_list]
            pool_weight = over(cut(deltas)) * jnp.exp(score_vals - over(cut(logs)))
            pool_grad = pool_weight.astype(jnp.bfloat16)
            score_grad = (pool_weight * (value_vals - over(cut(pools)))).astype(jnp.bfloat16)
            both = jnp.concatenate([score_grad, pool_grad], axis=1)
            sums = jnp.dot(turned, both, preferred_element_type=jnp.float32)
            for half in range(2):
                ready_ref[:, half * rows : (half + 1) * rows, codes] = (
                    sums[:, half * SPAN : (half + 1) * SPAN]
                    .astype(ready_ref.dtype)
                    .reshape(parts, rows, SPAN)
                )
            sent.append(
                pltpu.make_async_copy(
                    ready_ref.at[:, :, codes], grads_ref.at[:, :, codes], out_sems.at[len(sent)]
                )
            )
            sent[-1].start()
            key_grad += lax.dot_general(
                both,
                jnp.concatenate([query_blk, output_blk], axis=1),
                COLS,
                preferred_element_type=jnp.float32,
            )
        key_grad_ref[...] = key_grad.astype(key_grad_ref.dtype)
        for copy in sent:
            copy.wait()

    between = jnp.max(last - first) > 1
    heads = ids == first

    def ends(row_list):
        picked = []
        for end in (first, last):
            row = row_list[-1]
            for rec in range(records - 1):
                row = jnp.where(end == rec, row_list[rec], row)
            picked.append(row)
        return jnp.where(heads, *picked)

    pl.when(between)(lambda: apply(lambda row_list: spread(masks, row_list)))
    pl.when(jnp.logical_not(between))(lambda: apply(ends))


def pre_grad_kernel(parts_ref, keys_ref, out_ref):
    keys_f = keys_ref[...].astype(jnp.float32)
    total = jnp.sum(parts_ref[...].astype(jnp.float32), axis=0)
    own = (total * (1.0 - keys_f * keys_f)).astype(out_ref.dtype)
    out_ref[...] = jnp.broadcast_to(own[None], out_ref.shape)


def sum_kernel(parts_ref, out_ref):
    own = jnp.sum(parts_ref[...].astype(jnp.float32), axis=0).astype(out_ref.dtype)
    out_ref[...] = jnp.broadcast_to(own[None], out_ref.shape)


def final_kernel(
    grads_ref, weight_ref, loss_ref, grad_query_ref, grad_output_ref, grad_bias_ref, out_ref
):
    rows, records = grad_query_ref.shape[0], loss_ref.shape[0]
    grad_query_ref[...] = grads_ref[:rows].astype(jnp.float32)
    grad_output_ref[...] = grads_ref[rows : 2 * rows].astype(jnp.float32)
    shown = grads_ref[2 * rows :].astype(jnp.float32)
    loss_ref[...] = shown[:records] + shown[records : 2 * records]
    grad_bias_ref[...] = jnp.sum(shown[2 * records :], axis=0, keepdims=True)
    out_ref[...] = weight_ref[...].astype(jnp.float32)


def swap(parts, axis):
    return lax.all_to_all(parts, axis, 0, 0, tiled=True)


def struct(shape, dtype):
    return jax.ShapeDtypeStruct(shape, dtype)


def on_device(
    hidden_states, key_weight, queries, output_weight, code_bias, record_ids, code_labels
):
    f32, bf16 = jnp.float32, jnp.bfloat16
    records, width = code_labels.shape
    seq, label = lax.axis_size("seq"), lax.axis_size("label")
    tokens, feats = hidden_states.shape
    dims = key_weight.shape[1]
    rows = queries.shape[0]
    own_toks, own_feats = tokens // label, feats // seq

    few = pltpu.CompilerParams(vmem_limit_bytes=8 * 1024 * 1024)
    some = pltpu.CompilerParams(vmem_limit_bytes=50 * 1024 * 1024)
    many = pltpu.CompilerParams(vmem_limit_bytes=50 * 1024 * 1024)

    vectors = lax.all_gather(jnp.stack([queries, output_weight]), "seq", axis=0)
    partial_pre = jnp.dot(hidden_states, key_weight, preferred_element_type=f32)
    pre_parts = swap(partial_pre.reshape(label, own_toks, dims), "label")
    keys_own = jnp.tanh(jnp.sum(pre_parts, axis=0)).astype(bf16)
    keys_copies = jnp.broadcast_to(keys_own[None], (label, own_toks, dims))
    keys_all = swap(keys_copies, "label").reshape(tokens, dims)

    ids = record_ids[:, None]
    leader = (lax.axis_index("seq") == 0).astype(f32).reshape(1, 1)
    held = pl.BlockSpec(memory_space=pltpu.VMEM)
    far = pl.BlockSpec(memory_space=pltpu.HBM)
    blocks = width // SPAN
    own_totals, totals, vectors = pl.pallas_call(
        lambda *refs: totals_kernel(records, *refs),
        in_specs=[held, far, held],
        out_specs=[held, held, held],
        out_shape=[
            struct((2 * records, width), f32),
            struct((seq, 4, width + LANES), f32),
            struct(vectors.shape, bf16),
        ],
        scratch_shapes=[pltpu.SemaphoreType.DMA((blocks,))],
        compiler_params=many,
    )(keys_all, vectors, ids)
    totals = swap(totals, "seq")

    grads, key_grad = pl.pallas_call(
        lambda *refs: grads_kernel(records, *refs),
        in_specs=[held] * 8,
        out_specs=[far, held],
        out_shape=[
            struct((seq, 2 * rows + 4 * records, width), bf16),
            struct((tokens, dims), bf16),
        ],
        scratch_shapes=[
            pltpu.VMEM((seq, 2 * rows + 4 * records, width), bf16),
            pltpu.SemaphoreType.DMA((blocks,)),
        ],
        compiler_params=some,
    )(
        keys_all,
        vectors,
        ids,
        own_totals,
        totals,
        leader,
        code_bias[None],
        code_labels,
    )

    grads = lax.psum_scatter(grads, "seq", scatter_dimension=0)

    key_parts = swap(key_grad.reshape(label, own_toks, dims), "label")
    pre_copies = pl.pallas_call(
        pre_grad_kernel, out_shape=struct((label, own_toks, dims), bf16), compiler_params=few
    )(key_parts, keys_own)
    pre_grad = swap(pre_copies, "label").reshape(tokens, dims)
    weight_part = lax.dot_general(
        hidden_states, pre_grad, ROWS, preferred_element_type=f32
    ).astype(bf16)
    weight_parts = swap(weight_part.reshape(seq, own_feats, dims), "seq")
    weight_copies = pl.pallas_call(
        sum_kernel, out_shape=struct((seq, own_feats, dims), bf16), compiler_params=few
    )(weight_parts)
    weights = swap(weight_copies, "seq").reshape(feats, dims)
    code_loss, grad_queries, grad_output, grad_bias, grad_key_weight = pl.pallas_call(
        final_kernel,
        out_shape=[
            struct((records, width), f32),
            struct((rows, width), f32),
            struct((rows, width), f32),
            struct((1, width), f32),
            struct((feats, dims), f32),
        ],
        in_specs=[held, held],
        out_specs=[held] * 5,
        compiler_params=many,
    )(grads, weights)
    return (code_loss, grad_queries, grad_output, grad_bias[0], grad_key_weight)


def solution(mesh):
    return jax.shard_map(
        on_device,
        mesh=mesh,
        in_specs=(
            P("seq", "label"),
            P("label", None),
            P("seq", "label"),
            P("seq", "label"),
            P("label"),
            P("seq"),
            P(None, "label"),
        ),
        out_specs=(
            P(None, "label"),
            P("seq", "label"),
            P("seq", "label"),
            P("label"),
            P("label", None),
        ),
        check_vma=False,
    )
```
